32 devices in a mesh: store: 8 (over y, x, core), dept: 4 (over z).
Axes of the slice: x: 2, y: 2, z: 4, core: 2. Of those that a mesh axis runs over, the one named last changes fastest.
Arguments:
- history: bfloat16 [2048, 96, 512], P('store', 'dept'), may hold values from -400 to 400, as said below
- input_layer_matrix: bfloat16 [512, 512], replicated, may hold values from -0.375 to 0.375
- middle_layer_matrix: bfloat16 [512, 512], replicated, may hold values from -0.375 to 0.375
- final_layer_matrix: bfloat16 [512, 28], replicated, may hold values from -0.375 to 0.375
Outputs:
- reconciled: float32 [2048, 2688], P('store', 'dept')
- store_gap: float32 [28, 2048], P(None, 'store')
- item_gap: float32 [28, 96], P(None, 'dept')
The draws below stay inside these ranges and needn't reach their ends.
Inputs may be any that keep to these rules, and one draw needn't show every extreme that they name: `history`: daily sales histories.
All inputs are finite; a program needn't handle non-finite values.
Results may differ from the reference program's by a relative error of at most 0.0065.
The reference program's roundings to bfloat16 on the way count: a program that leaves them out, or rounds other values in their place, can miss the bound.
Values sent between devices are 32-bit elements; how exact they have to be, the bound alone decides.
A program may use at most 64 MiB of HBM per device.

```python
import math
import jax
import jax.numpy as jnp
from jax import lax

OUTLETS_IN_PIECE = 256
PAST_LENGTH = 512
HID = 512
AHEAD_LENGTH = 28
STORES = 2048
PRODUCT_NUMBER = 96


def draw_history(key, part):
    subkeys = jax.random.split(key, 4)
    store_scale = jnp.exp(jax.random.uniform(subkeys[0], (STORES,), jnp.float32, -1.15, 1.15))
    store_scale = store_scale * 3.0 ** (jnp.arange(STORES, dtype=jnp.float32) / STORES)
    item_scale = jnp.exp(jax.random.uniform(subkeys[1], (PRODUCT_NUMBER,), jnp.float32, -0.7, 0.7))
    item_scale = item_scale * 3.0 ** (jnp.arange(PRODUCT_NUMBER, dtype=jnp.float32) / PRODUCT_NUMBER)
    day_scale = jnp.exp(jax.random.uniform(subkeys[2], (PAST_LENGTH,), jnp.float32, -1.15, 1.15))
    jitter = jnp.clip(jax.random.normal(subkeys[3], (STORES, PRODUCT_NUMBER, PAST_LENGTH), jnp.float32), -4.0, 4.0)
    scaled = 0.3 * store_scale[:, None, None] * item_scale[None, :, None] * day_scale[None, None, :] * jitter
    return scaled.astype(jnp.bfloat16)


def scatter_about(rng, dims, width, limit, held_as=jnp.bfloat16):
    result = width * jax.random.normal(rng, dims, jnp.float32)
    return jnp.clip(result, min=-limit, max=limit).astype(held_as)


def setup_inputs(seed: int = 0) -> dict:
    key_list = jax.random.split(jax.random.key(seed), 5)
    history = draw_history(jax.random.fold_in(key_list[4], 71), 0)
    input_layer_matrix = scatter_about(key_list[1], (PAST_LENGTH, HID), (PAST_LENGTH // 2) ** -0.5, 0.375)
    middle_layer_matrix = scatter_about(key_list[2], (HID, HID), (HID // 2) ** -0.5, 0.375)
    final_layer_matrix = scatter_about(key_list[3], (HID, AHEAD_LENGTH), (HID // 2) ** -0.5, 0.375)
    return {"history": history, "input_layer_matrix": input_layer_matrix, "middle_layer_matrix": middle_layer_matrix, "final_layer_matrix": final_layer_matrix}


def predictor_function(sequence_grid, input_layer_matrix, middle_layer_matrix, final_layer_matrix):
    values = sequence_grid.astype(jnp.float32)
    root_mean = jnp.sqrt(lax.optimization_barrier(jnp.mean(values * values, axis=-1, keepdims=True)) + 1e-05)
    scaled = (values / root_mean).astype(jnp.bfloat16)
    hidden_one = jax.nn.relu(jnp.dot(scaled, input_layer_matrix, preferred_element_type=jnp.float32)).astype(jnp.bfloat16)
    hidden_two = jax.nn.relu(jnp.dot(hidden_one, middle_layer_matrix, preferred_element_type=jnp.float32)).astype(jnp.bfloat16)
    return jnp.dot(hidden_two, final_layer_matrix, preferred_element_type=jnp.float32) * root_mean

def reference(history, input_layer_matrix, middle_layer_matrix, final_layer_matrix):
    blocks = history.reshape(-1, OUTLETS_IN_PIECE, PRODUCT_NUMBER, PAST_LENGTH)

    def per_block(outlet_portion):
        projected_grid = predictor_function(outlet_portion.reshape(-1, PAST_LENGTH), input_layer_matrix, middle_layer_matrix, final_layer_matrix).reshape(OUTLETS_IN_PIECE, PRODUCT_NUMBER, AHEAD_LENGTH)
        widened_entries = outlet_portion.astype(jnp.float32)
        return (projected_grid, lax.optimization_barrier(jnp.sum(widened_entries, axis=1)), lax.optimization_barrier(jnp.sum(widened_entries, axis=0)))
    finest_tier, outlet_past_sales, item_parts = lax.map(per_block, blocks)
    finest_tier = finest_tier.reshape(STORES, PRODUCT_NUMBER, AHEAD_LENGTH)
    outlet_past_sales = outlet_past_sales.reshape(STORES, PAST_LENGTH)
    product_past_sales = lax.optimization_barrier(jnp.sum(item_parts, axis=0))
    outlet_estimate = predictor_function(outlet_past_sales, input_layer_matrix, middle_layer_matrix, final_layer_matrix)
    product_estimate = predictor_function(product_past_sales, input_layer_matrix, middle_layer_matrix, final_layer_matrix)
    row_sum = lax.optimization_barrier(jnp.sum(finest_tier, axis=1))
    col_sum = lax.optimization_barrier(jnp.sum(finest_tier, axis=0))
    store_err = outlet_estimate - row_sum
    item_err = product_estimate - col_sum
    err_s = lax.optimization_barrier(jnp.sum(store_err, axis=0))
    err_i = lax.optimization_barrier(jnp.sum(item_err, axis=0))
    item_count = float(PRODUCT_NUMBER)
    store_count = float(STORES)
    denominator = 1.0 + item_count + store_count
    shift_s = (err_s * (1.0 + store_count) - store_count * err_i) / denominator
    shift_i = ((1.0 + item_count) * err_i - item_count * err_s) / denominator
    store_shift = (store_err - shift_i) / (1.0 + item_count)
    item_shift = (item_err - shift_s) / (1.0 + store_count)
    reconciled = finest_tier + store_shift[:, None, :] + item_shift[None, :, :]
    store_gap = (store_err / math.sqrt(item_count)).T
    item_gap = (item_err / math.sqrt(store_count)).T
    return (reconciled.reshape(STORES, PRODUCT_NUMBER * AHEAD_LENGTH), store_gap, item_gap)
```

```python
import functools
import math

import jax
import jax.numpy as jnp
from jax import lax
from jax.experimental import pallas as pl
from jax.experimental.pallas import tpu as pltpu
from jax.sharding import PartitionSpec as P

MESH = pl.DeviceIdType.MESH
F32 = jnp.float32
BF16 = jnp.bfloat16
SLOT = 32
PACK = 4
STORES_IN_CHUNK = 32


def scales(values):
    mean = jnp.sum(values * values, axis=-1, keepdims=True) * (1.0 / values.shape[-1])
    return jnp.sqrt(mean + 1e-05)


def forecast(values, w1, w2, w3):
    root_mean = scales(values)
    scaled = (values * (1.0 / root_mean)).astype(BF16)
    one = jnp.maximum(jnp.dot(scaled, w1, preferred_element_type=F32).astype(BF16), 0)
    two = jnp.maximum(jnp.dot(one, w2, preferred_element_type=F32).astype(BF16), 0)
    return jnp.dot(two, w3, preferred_element_type=F32) * root_mean


def main_kernel(
    n_store, n_dept, stores, items, horizon,
    hist_hbm, w1_hbm, w2_hbm, w3_ref,
    base_out, store_shift_out, store_gap_out, item_shift_out, item_gap_out,
    hist, w1, w2, w3_wide, w3, selector, store_sums, store_recv, item_acc, item_sums, item_recv,
    sum_rows, flat, cs, cs_recv, ci, ci_recv, err, err_recv,
    hist_sem, weight_sem, ss_send, ss_get, is_send, is_get, cs_send, cs_get, ci_send, ci_get, err_send, err_get,
):
    my_store = lax.axis_index("store")
    my_dept = lax.axis_index("dept")
    total = n_store * n_dept
    me = my_store * n_dept + my_dept
    own = stores // n_dept
    own_rows = own * items
    days = hist.shape[1]
    item_share = item_sums.shape[1]
    groups = -(-items // PACK)
    dept_order = sorted(range(1, n_dept), key=lambda o: -min(o, n_dept - o)) + [0]

    def dept_at(off):
        return lax.rem(my_dept + off, n_dept)

    def store_at(off):
        return lax.rem(my_store + off, n_store)

    def device_at(off):
        there = lax.rem(me + off, total)
        return (there // n_dept, lax.rem(there, n_dept))

    def rows_of(chunk):
        return pl.ds(pl.multiple_of(chunk * own_rows, own_rows), own_rows)

    def load_chunk(off):
        rows = rows_of(dept_at(off))
        return pltpu.make_async_copy(hist_hbm.at[rows], hist.at[rows], hist_sem.at[off])

    for off in dept_order:
        load_chunk(off).start()
    load_w1 = pltpu.make_async_copy(w1_hbm, w1, weight_sem.at[0])
    load_w2 = pltpu.make_async_copy(w2_hbm, w2, weight_sem.at[1])
    load_w1.start()
    load_w2.start()

    barrier = pltpu.get_barrier_semaphore()

    def greet(off, carry):
        pl.semaphore_signal(barrier, inc=1, device_id=device_at(off), device_id_type=MESH)
        return carry

    lax.fori_loop(1, total, greet, 0)

    row = lax.broadcasted_iota(jnp.int32, selector.shape, 0)
    col = lax.broadcasted_iota(jnp.int32, selector.shape, 1)
    of_store = (col >= row * items) & (col < row * items + items)
    col_f = col.astype(F32)
    which = col_f - items * jnp.floor((col_f + 0.5) * (1.0 / items))
    of_item = which == (row - own).astype(F32)
    selector[...] = jnp.where(row < own, of_store.astype(F32), of_item.astype(F32)).astype(BF16)

    w3_wide[...] = jnp.zeros_like(w3_wide)
    last_layer = w3_ref[...].astype(F32)
    for j in range(PACK):
        w3_wide[j * SLOT:j * SLOT + horizon, :] = last_layer
    w3[...] = w3_wide[...].T.astype(BF16)

    pl.semaphore_wait(barrier, total - 1)

    def send_store(off):
        return pltpu.make_async_remote_copy(
            src_ref=store_sums.at[dept_at(off)], dst_ref=store_recv.at[off],
            send_sem=ss_send.at[off], recv_sem=ss_get.at[off],
            device_id=(my_store, dept_at(off)), device_id_type=MESH,
        )

    def send_item(off):
        return pltpu.make_async_remote_copy(
            src_ref=item_sums.at[store_at(off)], dst_ref=item_recv.at[off],
            send_sem=is_send.at[off], recv_sem=is_get.at[off],
            device_id=(store_at(off), my_dept), device_id_type=MESH,
        )

    item_total = None
    for off in dept_order:
        load_chunk(off).wait()
        sums = jnp.dot(selector[...], hist[rows_of(dept_at(off)), :], preferred_element_type=F32)
        store_sums[dept_at(off)] = sums[:own]
        if off:
            send_store(off).start()
        item_total = sums[own:] if item_total is None else item_total + sums[own:]
    item_acc[...] = jnp.zeros_like(item_acc)
    item_acc[0:items, :] = item_total
    for place in range(n_store):
        item_sums[place] = item_acc[place * item_share:(place + 1) * item_share, :]
    for off in range(1, n_store):
        send_item(off).start()

    load_w1.wait()
    load_w2.wait()
    rows_in_chunk = STORES_IN_CHUNK * items
    chunks = stores // STORES_IN_CHUNK
    half = 128
    lane = lax.broadcasted_iota(jnp.int32, (half, 128), 1)
    row_parts, col_parts = [], [None] * groups

    def chunk_step(chunk, carry):
        rows = pl.ds(pl.multiple_of(chunk * rows_in_chunk, rows_in_chunk), rows_in_chunk)
        flat[rows, :] = forecast(hist[rows, :].astype(F32), w1[...], w2[...], w3[...])
        return carry

    for part in range(stores // half):
        per = half // STORES_IN_CHUNK
        lax.fori_loop(part * per, (part + 1) * per, chunk_step, 0)
        row_part = None
        for k in range(groups):
            mixed = jnp.zeros((half, 128), F32)
            for j in range(PACK):
                if k * PACK + j < items:
                    one = flat[pl.ds(part * half * items + k * PACK + j, half, stride=items), :]
                    mixed = jnp.where((lane >= j * SLOT) & (lane < (j + 1) * SLOT), one, mixed)
            col_sum = jnp.sum(mixed, axis=0, keepdims=True)
            col_parts[k] = col_sum if col_parts[k] is None else col_parts[k] + col_sum
            turned = mixed.T
            base_out[k * 128:(k + 1) * 128, part * half:(part + 1) * half] = turned
            row_part = turned if row_part is None else row_part + turned
        row_parts.append(sum(row_part[j * SLOT:(j + 1) * SLOT] for j in range(PACK)))

    sum_rows[own:, :] = jnp.zeros((sum_rows.shape[0] - own, days), F32)
    store_total = store_sums[my_dept]
    for off in range(1, n_dept):
        send_store(off).wait()
        store_total = store_total + store_recv[off]
    sum_rows[0:own, :] = store_total
    item_total = item_sums[my_store]
    for off in range(1, n_store):
        send_item(off).wait()
        item_total = item_total + item_recv[off]
    sum_rows[own:own + item_share, :] = item_total
    upper = forecast(sum_rows[...], w1[...], w2[...], w3[...])
    wide = jnp.concatenate([upper[:own]] * n_dept, axis=0)
    place = lax.broadcasted_iota(jnp.int32, (SLOT, stores), 1)
    mine = (place >= my_dept * own) & (place < (my_dept + 1) * own)
    cs_mine = jnp.where(mine, wide.T[:SLOT], 0.0) - jnp.concatenate(row_parts, axis=1)
    cs[...] = cs_mine

    packed = lax.broadcasted_iota(jnp.int32, ci.shape, 0) * PACK
    packed_lane = lax.broadcasted_iota(jnp.int32, ci.shape, 1)
    for j in range(1, PACK):
        packed = packed + (packed_lane >= j * SLOT).astype(jnp.int32)
    ci[...] = jnp.zeros_like(ci)
    for k in range(groups):
        ci[k:k + 1, :] = 0.0 - col_parts[k]
    ci_mine = ci[...]
    for t in range(item_share):
        number = my_store * item_share + t
        ci_mine = ci_mine + jnp.where((packed == number) & (packed < items), upper[own + t:own + t + 1], 0.0)
    ci[...] = ci_mine

    def send_cs(off):
        return pltpu.make_async_remote_copy(
            src_ref=cs, dst_ref=cs_recv.at[off], send_sem=cs_send.at[off], recv_sem=cs_get.at[off],
            device_id=(my_store, dept_at(off)), device_id_type=MESH,
        )

    def send_ci(off):
        return pltpu.make_async_remote_copy(
            src_ref=ci, dst_ref=ci_recv.at[off], send_sem=ci_send.at[off], recv_sem=ci_get.at[off],
            device_id=(store_at(off), my_dept), device_id_type=MESH,
        )

    def send_err(off):
        return pltpu.make_async_remote_copy(
            src_ref=err, dst_ref=err_recv.at[off], send_sem=err_send.at[off], recv_sem=err_get.at[off],
            device_id=device_at(off), device_id_type=MESH,
        )

    for off in range(1, n_dept):
        send_cs(off).start()
    err_s_col = jnp.broadcast_to(jnp.sum(cs_mine, axis=1, keepdims=True), (SLOT, 128))
    err_s_mine = jnp.concatenate([err_s_col] * PACK, axis=0).T[0:1]
    err_i_mine = jnp.sum(ci_mine, axis=0, keepdims=True)
    err_i_mine = err_i_mine + pltpu.roll(err_i_mine, 2 * SLOT, 1)
    err_i_mine = err_i_mine + pltpu.roll(err_i_mine, SLOT, 1)
    err[0:1, :] = err_s_mine
    err[1:2, :] = err_i_mine

    def start_err(off, carry):
        send_err(off).start()
        return carry

    lax.fori_loop(1, total, start_err, 0)
    for off in range(1, n_store):
        send_ci(off).start()

    store_err = cs_mine
    for off in range(1, n_dept):
        send_cs(off).wait()
        store_err = store_err + cs_recv[off]
    item_err = ci_mine
    for off in range(1, n_store):
        send_ci(off).wait()
        item_err = item_err + ci_recv[off]

    def take_err(off, so_far):
        send_err(off).wait()
        return so_far + err_recv[off]

    errs = lax.fori_loop(1, total, take_err, err[...])
    err_s, err_i = errs[0:1], errs[1:2]
    item_count = float(items * n_dept)
    store_count = float(stores * n_store)
    denominator = 1.0 + item_count + store_count
    shift_s = (err_s * (1.0 + store_count) - store_count * err_i) / denominator
    shift_i = ((1.0 + item_count) * err_i - item_count * err_s) / denominator
    shift_i_col = jnp.broadcast_to(shift_i, (128, 128)).T[:SLOT]
    shift_i_all = jnp.concatenate([shift_i_col] * (stores // 128), axis=1)
    store_shift_out[...] = (store_err - shift_i_all) * (1.0 / (1.0 + item_count))
    store_gap_out[...] = store_err * (1.0 / math.sqrt(item_count))
    item_shift = (item_err - shift_s) * (1.0 / (1.0 + store_count))
    item_gap_out[...] = item_err * (1.0 / math.sqrt(store_count))
    padded = jnp.concatenate([item_shift] + [jnp.zeros((128 - item_shift.shape[0], 128), F32)], axis=0)
    item_shift_out[...] = padded.T


def final_kernel(
    items, horizon, base, store_shift, store_gap, item_shift, item_gap, reconciled_out, store_gap_out, item_gap_out
):
    shift = store_shift[...]
    for item in range(items):
        k, j = divmod(item, PACK)
        first = k * 128 + j * SLOT
        column = item_shift[j * SLOT:(j + 1) * SLOT, k:k + 1]
        block = base[first:first + SLOT, :] + shift + column
        reconciled_out[item * horizon:(item + 1) * horizon, :] = block[:horizon]
        item_gap_out[item:item + 1, :] = item_gap[k:k + 1, j * SLOT:j * SLOT + horizon]
    store_gap_out[...] = store_gap[0:horizon, :]


def body(n_store, n_dept, history, input_layer_matrix, middle_layer_matrix, final_layer_matrix):
    stores, items, days = history.shape
    hidden = input_layer_matrix.shape[1]
    horizon = final_layer_matrix.shape[1]
    own = stores // n_dept
    item_share = -(-items // n_store)
    groups = -(-items // PACK)
    group_rows = -(-groups // 8) * 8
    share_rows = -(-item_share // 8) * 8
    total = n_store * n_dept
    vmem = pl.BlockSpec(memory_space=pltpu.VMEM)
    anywhere = pl.BlockSpec(memory_space=pl.ANY)
    dma = pltpu.SemaphoreType.DMA
    shape = jax.ShapeDtypeStruct
    parts = pl.pallas_call(
        functools.partial(main_kernel, n_store, n_dept, stores, items, horizon),
        out_shape=(
            shape((groups * 128, stores), F32),
            shape((SLOT, stores), F32),
            shape((SLOT, stores), F32),
            shape((128, 128), F32),
            shape((group_rows, 128), F32),
        ),
        in_specs=[anywhere, anywhere, anywhere, vmem],
        out_specs=[vmem] * 5,
        scratch_shapes=[
            pltpu.VMEM((stores * items, days), BF16),
            pltpu.VMEM((days, hidden), BF16),
            pltpu.VMEM((hidden, hidden), BF16),
            pltpu.VMEM((128, hidden), F32),
            pltpu.VMEM((hidden, 128), BF16),
            pltpu.VMEM((own + items, own * items), BF16),
            pltpu.VMEM((n_dept, own, days), F32),
            pltpu.VMEM((n_dept, own, days), F32),
            pltpu.VMEM((-(-n_store * item_share // 8) * 8, days), F32),
            pltpu.VMEM((n_store, item_share, days), F32),
            pltpu.VMEM((n_store, item_share, days), F32),
            pltpu.VMEM((own + share_rows, days), F32),
            pltpu.VMEM((stores * items, 128), F32),
            pltpu.VMEM((SLOT, stores), F32),
            pltpu.VMEM((n_dept, SLOT, stores), F32),
            pltpu.VMEM((group_rows, 128), F32),
            pltpu.VMEM((n_store, group_rows, 128), F32),
            pltpu.VMEM((2, 128), F32),
            pltpu.VMEM((total, 2, 128), F32),
            dma((n_dept,)),
            dma((2,)),
            dma((n_dept,)),
            dma((n_dept,)),
            dma((n_store,)),
            dma((n_store,)),
            dma((n_dept,)),
            dma((n_dept,)),
            dma((n_store,)),
            dma((n_store,)),
            dma((total,)),
            dma((total,)),
        ],
        compiler_params=pltpu.CompilerParams(
            collective_id=0, has_side_effects=True, vmem_limit_bytes=40 * 2**20
        ),
    )(
        history.reshape(stores * items, days),
        input_layer_matrix,
        middle_layer_matrix,
        final_layer_matrix.T,
    )
    reconciled, store_gap, item_gap = pl.pallas_call(
        functools.partial(final_kernel, items, horizon),
        out_shape=(
            shape((items * horizon, stores), F32),
            shape((horizon, stores), F32),
            shape((items, horizon), F32),
        ),
        in_specs=[vmem] * 5,
        out_specs=[vmem] * 3,
        compiler_params=pltpu.CompilerParams(vmem_limit_bytes=16 * 2**20),
    )(*parts)
    return reconciled.T, store_gap, item_gap.T


def solution(mesh):
    return jax.shard_map(
        functools.partial(body, mesh.shape["store"], mesh.shape["dept"]),
        mesh=mesh,
        in_specs=(P("store", "dept", None), P(), P(), P()),
        out_specs=(P("store", "dept"), P(None, "store"), P(None, "dept")),
        check_vma=False,
    )
```

```python
import functools
import math

import jax
import jax.numpy as jnp
from jax import lax
from jax.experimental import pallas as pl
from jax.experimental.pallas import tpu as pltpu
from jax.sharding import PartitionSpec as P

MESH = pl.DeviceIdType.MESH
F32 = jnp.float32
BF16 = jnp.bfloat16
SLOT = 32
PACK = 4
STORES_IN_CHUNK = 32
SCALED_ROWS = 128


def scales(values):
    mean = jnp.sum(values * values, axis=-1, keepdims=True) * (1.0 / values.shape[-1])
    return jnp.sqrt(mean + 1e-05)


def forecast(values, w1, w2, w3):
    root_mean = scales(values)
    return layers((values * (1.0 / root_mean)).astype(BF16), w1, w2, w3) * root_mean


def layers(scaled, w1, w2, w3):
    one = jnp.maximum(jnp.dot(scaled, w1, preferred_element_type=F32).astype(BF16), 0)
    two = jnp.maximum(jnp.dot(one, w2, preferred_element_type=F32).astype(BF16), 0)
    return jnp.dot(two, w3, preferred_element_type=F32)


def main_kernel(
    n_store, n_dept, stores, items, horizon,
    hist_hbm, w1_hbm, w2_hbm, w3_hbm,
    base_out, small_out,
    base, small, hist, scaled, w1, w2, w3_narrow, w3_wide, w3, selector, store_sums, store_recv, item_acc, item_sums, item_recv,
    sum_rows, flat, cs, cs_recv, up, up_recv, ci, ci_recv, err, err_recv,
    hist_sem, weight_sem, ss_send, ss_get, is_send, is_get, cs_send, cs_get, up_send, up_get,
    ci_send, ci_get, err_send, err_get, out_sem,
):
    my_store = lax.axis_index("store")
    my_dept = lax.axis_index("dept")
    total = n_store * n_dept
    me = my_store * n_dept + my_dept
    own = stores // n_dept
    own_rows = own * items
    days = hist.shape[1]
    item_share = item_sums.shape[1]
    groups = -(-items // PACK)
    dept_order = sorted(range(1, n_dept), key=lambda o: -min(o, n_dept - o)) + [0]

    def dept_at(off):
        return lax.rem(my_dept + off, n_dept)

    def store_at(off):
        return lax.rem(my_store + off, n_store)

    def device_at(off):
        there = lax.rem(me + off, total)
        return (there // n_dept, lax.rem(there, n_dept))

    def rows_of(chunk):
        return pl.ds(pl.multiple_of(chunk * own_rows, own_rows), own_rows)

    def load_chunk(off):
        rows = rows_of(dept_at(off))
        return pltpu.make_async_copy(hist_hbm.at[rows], hist.at[rows], hist_sem.at[off])

    for off in dept_order:
        load_chunk(off).start()
    load_w1 = pltpu.make_async_copy(w1_hbm, w1, weight_sem.at[0])
    load_w2 = pltpu.make_async_copy(w2_hbm, w2, weight_sem.at[1])
    load_w3 = pltpu.make_async_copy(w3_hbm, w3_narrow, weight_sem.at[2])
    load_w3.start()
    load_w1.start()
    load_w2.start()

    barrier = pltpu.get_barrier_semaphore()

    def greet(off, carry):
        pl.semaphore_signal(barrier, inc=1, device_id=device_at(off), device_id_type=MESH)
        return carry

    lax.fori_loop(1, total, greet, 0)

    row = lax.broadcasted_iota(jnp.int32, selector.shape, 0)
    col = lax.broadcasted_iota(jnp.int32, selector.shape, 1)
    of_store = (col >= row * items) & (col < row * items + items)
    col_f = col.astype(F32)
    which = col_f - items * jnp.floor((col_f + 0.5) * (1.0 / items))
    of_item = which == (row - own).astype(F32)
    selector[...] = jnp.where(row < own, of_store.astype(F32), of_item.astype(F32)).astype(BF16)

    w3_wide[...] = jnp.zeros_like(w3_wide)
    load_w3.wait()
    last_layer = w3_narrow[...].astype(F32)
    for j in range(PACK):
        w3_wide[j * SLOT:j * SLOT + horizon, :] = last_layer
    w3[...] = w3_wide[...].T.astype(BF16)

    pl.semaphore_wait(barrier, total - 1)

    def send_store(off):
        return pltpu.make_async_remote_copy(
            src_ref=store_sums.at[dept_at(off)], dst_ref=store_recv.at[off],
            send_sem=ss_send.at[off], recv_sem=ss_get.at[off],
            device_id=(my_store, dept_at(off)), device_id_type=MESH,
        )

    def send_item(off):
        return pltpu.make_async_remote_copy(
            src_ref=item_sums.at[store_at(off)], dst_ref=item_recv.at[off],
            send_sem=is_send.at[off], recv_sem=is_get.at[off],
            device_id=(store_at(off), my_dept), device_id_type=MESH,
        )

    item_total = None
    for off in dept_order:
        load_chunk(off).wait()
        sums = jnp.dot(selector[...], hist[rows_of(dept_at(off)), :], preferred_element_type=F32)
        store_sums[dept_at(off)] = sums[:own]
        if off:
            send_store(off).start()
        item_total = sums[own:] if item_total is None else item_total + sums[own:]
        for first in range(0, own_rows, SCALED_ROWS):
            start = pl.multiple_of(dept_at(off) * own_rows + first, SCALED_ROWS)
            rows = pl.ds(start, SCALED_ROWS)
            root_mean = scales(hist[rows, :].astype(F32))
            flat[rows, :] = jnp.broadcast_to(root_mean, (SCALED_ROWS, 128))
            scaled[rows, :] = (hist[rows, :].astype(F32) * (1.0 / root_mean)).astype(BF16)
    item_acc[...] = jnp.zeros_like(item_acc)
    item_acc[0:items, :] = item_total
    for place in range(n_store):
        item_sums[place] = item_acc[place * item_share:(place + 1) * item_share, :]
    for off in range(1, n_store):
        send_item(off).start()

    load_w1.wait()
    load_w2.wait()
    rows_in_chunk = STORES_IN_CHUNK * items
    chunks = stores // STORES_IN_CHUNK
    half = 128
    lane = lax.broadcasted_iota(jnp.int32, (half, 128), 1)
    col_parts = [None] * groups

    def send_cs(off, part):
        return pltpu.make_async_remote_copy(
            src_ref=cs.at[part], dst_ref=cs_recv.at[off, part],
            send_sem=cs_send.at[off, part], recv_sem=cs_get.at[off, part],
            device_id=(my_store, dept_at(off)), device_id_type=MESH,
        )

    def send_up(off):
        return pltpu.make_async_remote_copy(
            src_ref=up, dst_ref=up_recv.at[off], send_sem=up_send.at[off], recv_sem=up_get.at[off],
            device_id=(my_store, dept_at(off)), device_id_type=MESH,
        )

    def chunk_step(chunk, carry):
        rows = pl.ds(pl.multiple_of(chunk * rows_in_chunk, rows_in_chunk), rows_in_chunk)
        flat[rows, :] = layers(scaled[rows, :], w1[...], w2[...], w3[...]) * flat[rows, :]
        return carry

    for part in range(stores // half):
        per = half // STORES_IN_CHUNK
        lax.fori_loop(part * per, (part + 1) * per, chunk_step, 0)
        row_part = None
        for k in range(groups):
            mixed = jnp.zeros((half, 128), F32)
            for j in range(PACK):
                if k * PACK + j < items:
                    one = flat[pl.ds(part * half * items + k * PACK + j, half, stride=items), :]
                    mixed = jnp.where((lane >= j * SLOT) & (lane < (j + 1) * SLOT), one, mixed)
            col_sum = jnp.sum(mixed, axis=0, keepdims=True)
            col_parts[k] = col_sum if col_parts[k] is None else col_parts[k] + col_sum
            turned = mixed.T
            base[k * 128:(k + 1) * 128, part * half:(part + 1) * half] = turned
            row_part = turned if row_part is None else row_part + turned
        cs[part] = sum(row_part[j * SLOT:(j + 1) * SLOT] for j in range(PACK))
        for off in dept_order[:-1]:
            send_cs(off, part).start()

    write_base = pltpu.make_async_copy(base, base_out, out_sem.at[0])
    write_base.start()

    sum_rows[own:, :] = jnp.zeros((sum_rows.shape[0] - own, days), F32)
    store_total = store_sums[my_dept]
    for off in range(1, n_dept):
        send_store(off).wait()
        store_total = store_total + store_recv[off]
    sum_rows[0:own, :] = store_total
    item_total = item_sums[my_store]
    for off in range(1, n_store):
        send_item(off).wait()
        item_total = item_total + item_recv[off]
    sum_rows[own:own + item_share, :] = item_total
    upper = forecast(sum_rows[...], w1[...], w2[...], w3[...])
    up[...] = jnp.concatenate([upper[:own]] * (128 // own), axis=0).T[:SLOT]
    for off in dept_order[:-1]:
        send_up(off).start()

    packed = lax.broadcasted_iota(jnp.int32, ci.shape, 0) * PACK
    packed_lane = lax.broadcasted_iota(jnp.int32, ci.shape, 1)
    for j in range(1, PACK):
        packed = packed + (packed_lane >= j * SLOT).astype(jnp.int32)
    ci[...] = jnp.zeros_like(ci)
    for k in range(groups):
        ci[k:k + 1, :] = 0.0 - col_parts[k]
    ci_mine = ci[...]
    for t in range(item_share):
        number = my_store * item_share + t
        ci_mine = ci_mine + jnp.where((packed == number) & (packed < items), upper[own + t:own + t + 1], 0.0)
    ci[...] = ci_mine

    def send_ci(off):
        return pltpu.make_async_remote_copy(
            src_ref=ci, dst_ref=ci_recv.at[off], send_sem=ci_send.at[off], recv_sem=ci_get.at[off],
            device_id=(store_at(off), my_dept), device_id_type=MESH,
        )

    def send_err(off):
        return pltpu.make_async_remote_copy(
            src_ref=err, dst_ref=err_recv.at[off], send_sem=err_send.at[off], recv_sem=err_get.at[off],
            device_id=device_at(off), device_id_type=MESH,
        )

    base_total = sum(col_parts)
    base_total = base_total + pltpu.roll(base_total, 2 * SLOT, 1)
    base_total = base_total + pltpu.roll(base_total, SLOT, 1)
    err[0:1, :] = jnp.sum(upper[:own], axis=0, keepdims=True) - base_total
    err[1:2, :] = jnp.sum(upper[own:own + item_share], axis=0, keepdims=True) - base_total

    def start_err(off, carry):
        send_err(off).start()
        return carry

    lax.fori_loop(1, total, start_err, 0)
    for off in range(1, n_store):
        send_ci(off).start()

    place = lax.broadcasted_iota(jnp.int32, (SLOT, stores), 1)

    def placed(piece, owner):
        mine = (place >= owner * own) & (place < (owner + 1) * own)
        return jnp.where(mine, jnp.concatenate([piece] * (stores // 128), axis=1), 0.0)

    store_parts = [cs[part] for part in range(stores // half)]
    store_err = placed(up[...], my_dept)
    for off in range(1, n_dept):
        for part in range(stores // half):
            send_cs(off, part).wait()
            store_parts[part] = store_parts[part] + cs_recv[off, part]
        send_up(off).wait()
        store_err = store_err + placed(up_recv[off], dept_at(n_dept - off))
    store_err = store_err - jnp.concatenate(store_parts, axis=1)
    item_err = ci_mine
    for off in range(1, n_store):
        send_ci(off).wait()
        item_err = item_err + ci_recv[off]

    def take_err(off, so_far):
        send_err(off).wait()
        return so_far + err_recv[off]

    errs = lax.fori_loop(1, total, take_err, err[...])
    err_s, err_i = errs[0:1], errs[1:2]
    item_count = float(items * n_dept)
    store_count = float(stores * n_store)
    denominator = 1.0 + item_count + store_count
    shift_s = (err_s * (1.0 + store_count) - store_count * err_i) / denominator
    shift_i = ((1.0 + item_count) * err_i - item_count * err_s) / denominator
    shift_i_col = jnp.broadcast_to(shift_i, (128, 128)).T[:SLOT]
    shift_i_all = jnp.concatenate([shift_i_col] * (stores // 128), axis=1)
    small[0:SLOT, :] = (store_err - shift_i_all) * (1.0 / (1.0 + item_count))
    small[SLOT:2 * SLOT, :] = store_err * (1.0 / math.sqrt(item_count))
    small[2 * SLOT:, 0:128] = (item_err - shift_s) * (1.0 / (1.0 + store_count))
    small[2 * SLOT:, 128:256] = item_err * (1.0 / math.sqrt(store_count))
    write_small = pltpu.make_async_copy(small, small_out, out_sem.at[1])
    write_small.start()
    write_base.wait()
    write_small.wait()


def final_kernel(items, horizon, base_hbm, small_hbm, reconciled_out, store_gap_out, item_gap_out, base, small, sem):
    read_small = pltpu.make_async_copy(small_hbm, small, sem.at[0])
    read_base = pltpu.make_async_copy(base_hbm, base, sem.at[1])
    read_small.start()
    read_base.start()
    read_small.wait()
    shift = small[0:SLOT, :]
    store_gap_out[...] = small[SLOT:SLOT + horizon, :]
    item_shift = small[2 * SLOT:, 0:128]
    item_gap = small[2 * SLOT:, 128:256]
    columns = jnp.concatenate([item_shift] + [jnp.zeros((128 - item_shift.shape[0], 128), F32)], axis=0).T
    read_base.wait()
    for item in range(items):
        k, j = divmod(item, PACK)
        first = k * 128 + j * SLOT
        block = base[first:first + SLOT, :] + shift + columns[j * SLOT:(j + 1) * SLOT, k:k + 1]
        reconciled_out[item * horizon:(item + 1) * horizon, :] = block[:horizon]
        item_gap_out[item:item + 1, :] = item_gap[k:k + 1, j * SLOT:j * SLOT + horizon]


def body(n_store, n_dept, history, input_layer_matrix, middle_layer_matrix, final_layer_matrix):
    stores, items, days = history.shape
    hidden = input_layer_matrix.shape[1]
    horizon = final_layer_matrix.shape[1]
    own = stores // n_dept
    item_share = -(-items // n_store)
    groups = -(-items // PACK)
    group_rows = -(-groups // 8) * 8
    share_rows = -(-item_share // 8) * 8
    total = n_store * n_dept
    vmem = pl.BlockSpec(memory_space=pltpu.VMEM)
    in_hbm = pl.BlockSpec(memory_space=pl.ANY)
    dma = pltpu.SemaphoreType.DMA
    shape = jax.ShapeDtypeStruct
    parts = pl.pallas_call(
        functools.partial(main_kernel, n_store, n_dept, stores, items, horizon),
        out_shape=(
            shape((groups * 128, stores), F32),
            shape((2 * SLOT + group_rows, stores), F32),
        ),
        in_specs=[in_hbm] * 4,
        out_specs=[in_hbm] * 2,
        scratch_shapes=[
            pltpu.VMEM((groups * 128, stores), F32),
            pltpu.VMEM((2 * SLOT + group_rows, stores), F32),
            pltpu.VMEM((stores * items, days), BF16),
            pltpu.VMEM((stores * items, days), BF16),
            pltpu.VMEM((days, hidden), BF16),
            pltpu.VMEM((hidden, hidden), BF16),
            pltpu.VMEM((horizon, hidden), BF16),
            pltpu.VMEM((128, hidden), F32),
            pltpu.VMEM((hidden, 128), BF16),
            pltpu.VMEM((own + items, own * items), BF16),
            pltpu.VMEM((n_dept, own, days), F32),
            pltpu.VMEM((n_dept, own, days), F32),
            pltpu.VMEM((-(-n_store * item_share // 8) * 8, days), F32),
            pltpu.VMEM((n_store, item_share, days), F32),
            pltpu.VMEM((n_store, item_share, days), F32),
            pltpu.VMEM((own + share_rows, days), F32),
            pltpu.VMEM((stores * items, 128), F32),
            pltpu.VMEM((stores // 128, SLOT, 128), F32),
            pltpu.VMEM((n_dept, stores // 128, SLOT, 128), F32),
            pltpu.VMEM((SLOT, 128), F32),
            pltpu.VMEM((n_dept, SLOT, 128), F32),
            pltpu.VMEM((group_rows, 128), F32),
            pltpu.VMEM((n_store, group_rows, 128), F32),
            pltpu.VMEM((2, 128), F32),
            pltpu.VMEM((total, 2, 128), F32),
            dma((n_dept,)),
            dma((3,)),
            dma((n_dept,)),
            dma((n_dept,)),
            dma((n_store,)),
            dma((n_store,)),
            dma((n_dept, stores // 128)),
            dma((n_dept, stores // 128)),
            dma((n_dept,)),
            dma((n_dept,)),
            dma((n_store,)),
            dma((n_store,)),
            dma((total,)),
            dma((total,)),
            dma((2,)),
        ],
        compiler_params=pltpu.CompilerParams(
            collective_id=0, has_side_effects=True, vmem_limit_bytes=60 * 2**20
        ),
    )(
        history.reshape(stores * items, days),
        input_layer_matrix,
        middle_layer_matrix,
        final_layer_matrix.T,
    )
    reconciled, store_gap, item_gap = pl.pallas_call(
        functools.partial(final_kernel, items, horizon),
        out_shape=(
            shape((items * horizon, stores), F32),
            shape((horizon, stores), F32),
            shape((items, horizon), F32),
        ),
        in_specs=[in_hbm] * 2,
        out_specs=[vmem] * 3,
        scratch_shapes=[
            pltpu.VMEM((groups * 128, stores), F32),
            pltpu.VMEM((2 * SLOT + group_rows, stores), F32),
            dma((2,)),
        ],
        compiler_params=pltpu.CompilerParams(vmem_limit_bytes=60 * 2**20),
    )(*parts)
    return reconciled.T, store_gap, item_gap.T


def solution(mesh):
    return jax.shard_map(
        functools.partial(body, mesh.shape["store"], mesh.shape["dept"]),
        mesh=mesh,
        in_specs=(P("store", "dept", None), P(), P(), P()),
        out_specs=(P("store", "dept"), P(None, "store"), P(None, "dept")),
        check_vma=False,
    )
```

```python
import functools
import math

import jax
import jax.numpy as jnp
from jax import lax
from jax.experimental import pallas as pl
from jax.experimental.pallas import tpu as pltpu
from jax.sharding import PartitionSpec as P

MESH = pl.DeviceIdType.MESH
F32 = jnp.float32
BF16 = jnp.bfloat16
SLOT = 32
PACK = 4
STORES_IN_CHUNK = 32
SCALED_ROWS = 128


def scales(values):
    mean = jnp.sum(values * values, axis=-1, keepdims=True) * (1.0 / values.shape[-1])
    return jnp.sqrt(mean + 1e-05)


def layers(blocks, w1, w2, w3):
    for weights in (w1, w2):
        blocks = [jnp.dot(block, weights[...], preferred_element_type=F32).astype(BF16) for block in blocks]
        blocks = [jnp.maximum(block, 0) for block in blocks]
    return [jnp.dot(block, w3[...], preferred_element_type=F32) for block in blocks]


def main_kernel(
    n_store, n_dept, stores, items, horizon,
    hist_hbm, w1_hbm, w2_hbm, w3_hbm,
    base_out, small_out,
    base, small, hist, scaled, w1, w2, w3_narrow, w3_wide, w3, selector, store_sums, store_recv, item_acc, item_sums, item_recv,
    sum_rows, flat, cs, cs_recv, up, up_recv, ci, ci_recv, err, err_recv,
    hist_sem, weight_sem, ss_send, ss_get, is_send, is_get, cs_send, cs_get, up_send, up_get,
    ci_send, ci_get, err_send, err_get, out_sem,
):
    my_store = lax.axis_index("store")
    my_dept = lax.axis_index("dept")
    total = n_store * n_dept
    me = my_store * n_dept + my_dept
    own = stores // n_dept
    own_rows = own * items
    days = hist.shape[1]
    item_share = item_sums.shape[1]
    groups = -(-items // PACK)
    dept_order = sorted(range(1, n_dept), key=lambda o: -min(o, n_dept - o)) + [0]

    def dept_at(off):
        return lax.rem(my_dept + off, n_dept)

    def store_at(off):
        return lax.rem(my_store + off, n_store)

    def device_at(off):
        there = lax.rem(me + off, total)
        return (there // n_dept, lax.rem(there, n_dept))

    def rows_of(chunk):
        return pl.ds(pl.multiple_of(chunk * own_rows, own_rows), own_rows)

    def load_chunk(off):
        rows = rows_of(dept_at(off))
        return pltpu.make_async_copy(hist_hbm.at[rows], hist.at[rows], hist_sem.at[off])

    for off in dept_order:
        load_chunk(off).start()
    load_w1 = pltpu.make_async_copy(w1_hbm, w1, weight_sem.at[0])
    load_w2 = pltpu.make_async_copy(w2_hbm, w2, weight_sem.at[1])
    load_w3 = pltpu.make_async_copy(w3_hbm, w3_narrow, weight_sem.at[2])
    load_w3.start()
    load_w1.start()
    load_w2.start()

    barrier = pltpu.get_barrier_semaphore()

    def greet(off, carry):
        pl.semaphore_signal(barrier, inc=1, device_id=device_at(off), device_id_type=MESH)
        return carry

    lax.fori_loop(1, total, greet, 0)

    row = lax.broadcasted_iota(jnp.int32, selector.shape, 0)
    col = lax.broadcasted_iota(jnp.int32, selector.shape, 1)
    of_store = (col >= row * items) & (col < row * items + items)
    col_f = col.astype(F32)
    which = col_f - items * jnp.floor((col_f + 0.5) * (1.0 / items))
    of_item = which == (row - own).astype(F32)
    selector[...] = jnp.where(row < own, of_store.astype(F32), of_item.astype(F32)).astype(BF16)

    w3_wide[...] = jnp.zeros_like(w3_wide)
    load_w3.wait()
    last_layer = w3_narrow[...].astype(F32)
    for j in range(PACK):
        w3_wide[j * SLOT:j * SLOT + horizon, :] = last_layer
    w3[...] = w3_wide[...].T.astype(BF16)

    pl.semaphore_wait(barrier, total - 1)

    def send_store(off):
        return pltpu.make_async_remote_copy(
            src_ref=store_sums.at[dept_at(off)], dst_ref=store_recv.at[off],
            send_sem=ss_send.at[off], recv_sem=ss_get.at[off],
            device_id=(my_store, dept_at(off)), device_id_type=MESH,
        )

    def send_item(off):
        return pltpu.make_async_remote_copy(
            src_ref=item_sums.at[store_at(off)], dst_ref=item_recv.at[off],
            send_sem=is_send.at[off], recv_sem=is_get.at[off],
            device_id=(store_at(off), my_dept), device_id_type=MESH,
        )

    item_total = None
    for off in dept_order:
        load_chunk(off).wait()
        sums = jnp.dot(selector[...], hist[rows_of(dept_at(off)), :], preferred_element_type=F32)
        store_sums[dept_at(off)] = sums[:own]
        if off:
            send_store(off).start()
        item_total = sums[own:] if item_total is None else item_total + sums[own:]
    item_acc[...] = jnp.zeros_like(item_acc)
    item_acc[0:items, :] = item_total
    for place in range(n_store):
        item_sums[place] = item_acc[place * item_share:(place + 1) * item_share, :]
    for off in range(1, n_store):
        send_item(off).start()

    load_w1.wait()
    load_w2.wait()
    half = 128
    lane = lax.broadcasted_iota(jnp.int32, (half, 128), 1)
    col_parts = [None] * groups

    def send_cs(off, part):
        return pltpu.make_async_remote_copy(
            src_ref=cs.at[part], dst_ref=cs_recv.at[off, part],
            send_sem=cs_send.at[off, part], recv_sem=cs_get.at[off, part],
            device_id=(my_store, dept_at(off)), device_id_type=MESH,
        )

    def send_up(off):
        return pltpu.make_async_remote_copy(
            src_ref=up, dst_ref=up_recv.at[off], send_sem=up_send.at[off], recv_sem=up_get.at[off],
            device_id=(my_store, dept_at(off)), device_id_type=MESH,
        )

    def scale(first, count):
        for start in range(first, first + count, SCALED_ROWS):
            rows = slice(start, start + SCALED_ROWS)
            root_mean = scales(hist[rows, :].astype(F32))
            flat[rows, :] = jnp.broadcast_to(root_mean, (SCALED_ROWS, 128))
            scaled[rows, :] = (hist[rows, :].astype(F32) * (1.0 / root_mean)).astype(BF16)

    def run(first, sizes, more=()):
        starts = [first + sum(sizes[:i]) for i in range(len(sizes))]
        pieces = [slice(start, start + size) for start, size in zip(starts, sizes)]
        results = layers(list(more) + [scaled[rows, :] for rows in pieces], w1, w2, w3)
        for rows, result in zip(pieces, results[len(more):]):
            flat[rows, :] = result * flat[rows, :]
        return results[:len(more)]

    def turn(part):
        row_part = None
        for k in range(groups):
            mixed = jnp.zeros((half, 128), F32)
            for j in range(PACK):
                if k * PACK + j < items:
                    one = flat[pl.ds(part * half * items + k * PACK + j, half, stride=items), :]
                    mixed = jnp.where((lane >= j * SLOT) & (lane < (j + 1) * SLOT), one, mixed)
            col_sum = jnp.sum(mixed, axis=0, keepdims=True)
            col_parts[k] = col_sum if col_parts[k] is None else col_parts[k] + col_sum
            turned = mixed.T
            base[k * 128:(k + 1) * 128, part * half:(part + 1) * half] = turned
            row_part = turned if row_part is None else row_part + turned
        cs[part] = sum(row_part[j * SLOT:(j + 1) * SLOT] for j in range(PACK))
        for off in dept_order[:-1]:
            send_cs(off, part).start()

    block = STORES_IN_CHUNK * items
    blocks = stores // STORES_IN_CHUNK
    blocks_in_half = half // STORES_IN_CHUNK
    scale(0, 2 * block)
    for number in range(0, blocks - 2, 2):
        run(number * block, [block, block])
        scale((number + 2) * block, 2 * block)
        if (number + 2) % blocks_in_half == 0:
            turn((number + 2) // blocks_in_half - 1)

    sum_rows[own:, :] = jnp.zeros((sum_rows.shape[0] - own, days), F32)
    store_total = store_sums[my_dept]
    for off in range(1, n_dept):
        send_store(off).wait_recv()
        store_total = store_total + store_recv[off]
    sum_rows[0:own, :] = store_total
    item_total = item_sums[my_store]
    for off in range(1, n_store):
        send_item(off).wait_recv()
        item_total = item_total + item_recv[off]
    sum_rows[own:own + item_share, :] = item_total
    upper_mean = scales(sum_rows[...])
    upper_scaled = (sum_rows[...] * (1.0 / upper_mean)).astype(BF16)
    (upper,) = run((blocks - 2) * block, [block], [upper_scaled])
    upper = upper * upper_mean
    up[...] = jnp.concatenate([upper[:own]] * (128 // own), axis=0).T[:SLOT]
    for off in dept_order[:-1]:
        send_up(off).start()

    run((blocks - 1) * block, [block // 2, block // 2])
    turn(stores // half - 1)
    write_base = pltpu.make_async_copy(base, base_out, out_sem.at[0])
    write_base.start()

    packed = lax.broadcasted_iota(jnp.int32, ci.shape, 0) * PACK
    packed_lane = lax.broadcasted_iota(jnp.int32, ci.shape, 1)
    for j in range(1, PACK):
        packed = packed + (packed_lane >= j * SLOT).astype(jnp.int32)
    ci[...] = jnp.zeros_like(ci)
    for k in range(groups):
        ci[k:k + 1, :] = 0.0 - col_parts[k]
    ci_mine = ci[...]
    for t in range(item_share):
        number = my_store * item_share + t
        ci_mine = ci_mine + jnp.where((packed == number) & (packed < items), upper[own + t:own + t + 1], 0.0)
    ci[...] = ci_mine

    def send_ci(off):
        return pltpu.make_async_remote_copy(
            src_ref=ci, dst_ref=ci_recv.at[off], send_sem=ci_send.at[off], recv_sem=ci_get.at[off],
            device_id=(store_at(off), my_dept), device_id_type=MESH,
        )

    def send_err(off):
        return pltpu.make_async_remote_copy(
            src_ref=err, dst_ref=err_recv.at[off], send_sem=err_send.at[off], recv_sem=err_get.at[off],
            device_id=device_at(off), device_id_type=MESH,
        )

    base_total = sum(col_parts)
    base_total = base_total + pltpu.roll(base_total, 2 * SLOT, 1)
    base_total = base_total + pltpu.roll(base_total, SLOT, 1)
    err[0:1, :] = jnp.sum(upper[:own], axis=0, keepdims=True) - base_total
    err[1:2, :] = jnp.sum(upper[own:own + item_share], axis=0, keepdims=True) - base_total

    def start_err(off, carry):
        send_err(off).start()
        return carry

    lax.fori_loop(1, total, start_err, 0)
    for off in range(1, n_store):
        send_ci(off).start()

    place = lax.broadcasted_iota(jnp.int32, (SLOT, stores), 1)

    def placed(piece, owner):
        mine = (place >= owner * own) & (place < (owner + 1) * own)
        return jnp.where(mine, jnp.concatenate([piece] * (stores // 128), axis=1), 0.0)

    store_parts = [cs[part] for part in range(stores // half)]
    store_err = placed(up[...], my_dept)
    for off in range(1, n_dept):
        for part in range(stores // half):
            send_cs(off, part).wait_recv()
            store_parts[part] = store_parts[part] + cs_recv[off, part]
        send_up(off).wait_recv()
        store_err = store_err + placed(up_recv[off], dept_at(n_dept - off))
    store_err = store_err - jnp.concatenate(store_parts, axis=1)
    item_err = ci_mine
    for off in range(1, n_store):
        send_ci(off).wait_recv()
        item_err = item_err + ci_recv[off]

    def take_err(off, so_far):
        send_err(off).wait_recv()
        return so_far + err_recv[off]

    errs = lax.fori_loop(1, total, take_err, err[...])
    err_s, err_i = errs[0:1], errs[1:2]
    item_count = float(items * n_dept)
    store_count = float(stores * n_store)
    denominator = 1.0 + item_count + store_count
    shift_s = (err_s * (1.0 + store_count) - store_count * err_i) / denominator
    shift_i = ((1.0 + item_count) * err_i - item_count * err_s) / denominator
    shift_i_col = jnp.broadcast_to(shift_i, (128, 128)).T[:SLOT]
    shift_i_all = jnp.concatenate([shift_i_col] * (stores // 128), axis=1)
    small[0:SLOT, :] = (store_err - shift_i_all) * (1.0 / (1.0 + item_count))
    small[SLOT:2 * SLOT, :] = store_err * (1.0 / math.sqrt(item_count))
    small[2 * SLOT:, 0:128] = (item_err - shift_s) * (1.0 / (1.0 + store_count))
    small[2 * SLOT:, 128:256] = item_err * (1.0 / math.sqrt(store_count))
    write_small = pltpu.make_async_copy(small, small_out, out_sem.at[1])
    write_small.start()

    def leave_err(off, carry):
        send_err(off).wait_send()
        return carry

    for off in range(1, n_dept):
        send_store(off).wait_send()
        send_up(off).wait_send()
        for part in range(stores // half):
            send_cs(off, part).wait_send()
    for off in range(1, n_store):
        send_item(off).wait_send()
        send_ci(off).wait_send()
    lax.fori_loop(1, total, leave_err, 0)
    write_base.wait()
    write_small.wait()


def final_kernel(
    items, horizon, base_hbm, small_hbm, reconciled_out, store_gap_out, item_gap_out,
    base, small, reconciled, store_gap, item_gap, read_sem, write_sem,
):
    groups = base.shape[0] // 128
    read_small = pltpu.make_async_copy(small_hbm, small, read_sem.at[groups])
    read_small.start()
    reads, writes = [], []
    for k in range(groups):
        rows = pl.ds(k * 128, 128)
        reads.append(pltpu.make_async_copy(base_hbm.at[rows], base.at[rows], read_sem.at[k]))
        reads[k].start()
    read_small.wait()
    shift = small[0:SLOT, :]
    item_shift = small[2 * SLOT:, 0:128]
    gap = small[2 * SLOT:, 128:256]
    columns = jnp.concatenate([item_shift] + [jnp.zeros((128 - item_shift.shape[0], 128), F32)], axis=0).T
    store_gap[...] = small[SLOT:SLOT + horizon, :]
    for item in range(items):
        k, j = divmod(item, PACK)
        item_gap[item:item + 1, :] = gap[k:k + 1, j * SLOT:j * SLOT + horizon]
    writes.append(pltpu.make_async_copy(store_gap, store_gap_out, write_sem.at[groups]))
    writes.append(pltpu.make_async_copy(item_gap, item_gap_out, write_sem.at[groups + 1]))
    writes[0].start()
    writes[1].start()
    for k in range(groups):
        reads[k].wait()
        mine = range(k * PACK, min((k + 1) * PACK, items))
        for item in mine:
            j = item - k * PACK
            first = k * 128 + j * SLOT
            block = base[first:first + SLOT, :] + shift + columns[j * SLOT:(j + 1) * SLOT, k:k + 1]
            reconciled[item * horizon:(item + 1) * horizon, :] = block[:horizon]
        rows = pl.ds(mine[0] * horizon, len(mine) * horizon)
        writes.append(pltpu.make_async_copy(reconciled.at[rows], reconciled_out.at[rows], write_sem.at[k]))
        writes[-1].start()
    for write in writes:
        write.wait()


def body(n_store, n_dept, history, input_layer_matrix, middle_layer_matrix, final_layer_matrix):
    stores, items, days = history.shape
    hidden = input_layer_matrix.shape[1]
    horizon = final_layer_matrix.shape[1]
    own = stores // n_dept
    item_share = -(-items // n_store)
    groups = -(-items // PACK)
    group_rows = -(-groups // 8) * 8
    share_rows = -(-item_share // 8) * 8
    total = n_store * n_dept
    in_hbm = pl.BlockSpec(memory_space=pl.ANY)
    dma = pltpu.SemaphoreType.DMA
    shape = jax.ShapeDtypeStruct
    parts = pl.pallas_call(
        functools.partial(main_kernel, n_store, n_dept, stores, items, horizon),
        out_shape=(
            shape((groups * 128, stores), F32),
            shape((2 * SLOT + group_rows, stores), F32),
        ),
        in_specs=[in_hbm] * 4,
        out_specs=[in_hbm] * 2,
        scratch_shapes=[
            pltpu.VMEM((groups * 128, stores), F32),
            pltpu.VMEM((2 * SLOT + group_rows, stores), F32),
            pltpu.VMEM((stores * items, days), BF16),
            pltpu.VMEM((stores * items, days), BF16),
            pltpu.VMEM((days, hidden), BF16),
            pltpu.VMEM((hidden, hidden), BF16),
            pltpu.VMEM((horizon, hidden), BF16),
            pltpu.VMEM((128, hidden), F32),
            pltpu.VMEM((hidden, 128), BF16),
            pltpu.VMEM((own + items, own * items), BF16),
            pltpu.VMEM((n_dept, own, days), F32),
            pltpu.VMEM((n_dept, own, days), F32),
            pltpu.VMEM((-(-n_store * item_share // 8) * 8, days), F32),
            pltpu.VMEM((n_store, item_share, days), F32),
            pltpu.VMEM((n_store, item_share, days), F32),
            pltpu.VMEM((own + share_rows, days), F32),
            pltpu.VMEM((stores * items, 128), F32),
            pltpu.VMEM((stores // 128, SLOT, 128), F32),
            pltpu.VMEM((n_dept, stores // 128, SLOT, 128), F32),
            pltpu.VMEM((SLOT, 128), F32),
            pltpu.VMEM((n_dept, SLOT, 128), F32),
            pltpu.VMEM((group_rows, 128), F32),
            pltpu.VMEM((n_store, group_rows, 128), F32),
            pltpu.VMEM((2, 128), F32),
            pltpu.VMEM((total, 2, 128), F32),
            dma((n_dept,)),
            dma((3,)),
            dma((n_dept,)),
            dma((n_dept,)),
            dma((n_store,)),
            dma((n_store,)),
            dma((n_dept, stores // 128)),
            dma((n_dept, stores // 128)),
            dma((n_dept,)),
            dma((n_dept,)),
            dma((n_store,)),
            dma((n_store,)),
            dma((total,)),
            dma((total,)),
            dma((2,)),
        ],
        compiler_params=pltpu.CompilerParams(
            collective_id=0, has_side_effects=True, vmem_limit_bytes=60 * 2**20
        ),
    )(
        history.reshape(stores * items, days),
        input_layer_matrix,
        middle_layer_matrix,
        final_layer_matrix.T,
    )
    reconciled, store_gap, item_gap = pl.pallas_call(
        functools.partial(final_kernel, items, horizon),
        out_shape=(
            shape((items * horizon, stores), F32),
            shape((horizon, stores), F32),
            shape((items, horizon), F32),
        ),
        in_specs=[in_hbm] * 2,
        out_specs=[in_hbm] * 3,
        scratch_shapes=[
            pltpu.VMEM((groups * 128, stores), F32),
            pltpu.VMEM((2 * SLOT + group_rows, stores), F32),
            pltpu.VMEM((items * horizon, stores), F32),
            pltpu.VMEM((horizon, stores), F32),
            pltpu.VMEM((items, horizon), F32),
            dma((groups + 1,)),
            dma((groups + 2,)),
        ],
        compiler_params=pltpu.CompilerParams(vmem_limit_bytes=60 * 2**20),
    )(*parts)
    return reconciled.T, store_gap, item_gap.T


def solution(mesh):
    return jax.shard_map(
        functools.partial(body, mesh.shape["store"], mesh.shape["dept"]),
        mesh=mesh,
        in_specs=(P("store", "dept", None), P(), P(), P()),
        out_specs=(P("store", "dept"), P(None, "store"), P(None, "dept")),
        check_vma=False,
    )
```

```python
import functools
import math

import jax
import jax.numpy as jnp
from jax import lax
from jax.experimental import pallas as pl
from jax.experimental.pallas import tpu as pltpu
from jax.sharding import PartitionSpec as P

MESH = pl.DeviceIdType.MESH
F32 = jnp.float32
BF16 = jnp.bfloat16
SLOT = 32
PACK = 4
STORES_IN_CHUNK = 32
SCALED_ROWS = 128


def scales(values):
    mean = jnp.sum(values * values, axis=-1, keepdims=True) * (1.0 / values.shape[-1])
    return jnp.sqrt(mean + 1e-05)


def layers(blocks, w1, w2, w3):
    for weights in (w1, w2):
        blocks = [jnp.dot(block, weights[...], preferred_element_type=F32).astype(BF16) for block in blocks]
        blocks = [jnp.maximum(block, 0) for block in blocks]
    return [jnp.dot(block, w3[...], preferred_element_type=F32) for block in blocks]


def main_kernel(
    n_store, n_dept, stores, items, horizon,
    hist_hbm, w1_hbm, w2_hbm, w3_hbm,
    base_out, small_out,
    base, small, hist, scaled, w1, w2, w3_narrow, w3_wide, w3, selector, store_sums, store_recv, item_acc, item_sums, item_recv,
    sum_rows, flat, cs, cs_recv, up, up_recv, ci, ci_recv, err, err_recv,
    hist_sem, weight_sem, ss_send, ss_get, is_send, is_get, cs_send, cs_get, up_send, up_get,
    ci_send, ci_get, err_send, err_get, out_sem,
):
    my_store = lax.axis_index("store")
    my_dept = lax.axis_index("dept")
    own = stores // n_dept
    own_rows = own * items
    days = hist.shape[1]
    item_share = item_sums.shape[1]
    groups = -(-items // PACK)
    dept_order = sorted(range(1, n_dept), key=lambda o: -min(o, n_dept - o)) + [0]

    def dept_at(off):
        return lax.rem(my_dept + off, n_dept)

    def store_at(off):
        return lax.rem(my_store + off, n_store)

    def rows_of(chunk):
        return pl.ds(pl.multiple_of(chunk * own_rows, own_rows), own_rows)

    def load_chunk(off):
        rows = rows_of(dept_at(off))
        return pltpu.make_async_copy(hist_hbm.at[rows], hist.at[rows], hist_sem.at[off])

    for off in dept_order:
        load_chunk(off).start()
    load_w1 = pltpu.make_async_copy(w1_hbm, w1, weight_sem.at[0])
    load_w2 = pltpu.make_async_copy(w2_hbm, w2, weight_sem.at[1])
    load_w3 = pltpu.make_async_copy(w3_hbm, w3_narrow, weight_sem.at[2])
    load_w3.start()
    load_w1.start()
    load_w2.start()

    barrier = pltpu.get_barrier_semaphore()

    for off in range(1, n_dept):
        pl.semaphore_signal(barrier, inc=1, device_id=(my_store, dept_at(off)), device_id_type=MESH)
    for off in range(1, n_store):
        pl.semaphore_signal(barrier, inc=1, device_id=(store_at(off), my_dept), device_id_type=MESH)

    row = lax.broadcasted_iota(jnp.int32, selector.shape, 0)
    col = lax.broadcasted_iota(jnp.int32, selector.shape, 1)
    of_store = (col >= row * items) & (col < row * items + items)
    col_f = col.astype(F32)
    which = col_f - items * jnp.floor((col_f + 0.5) * (1.0 / items))
    of_item = which == (row - own).astype(F32)
    selector[...] = jnp.where(row < own, of_store.astype(F32), of_item.astype(F32)).astype(BF16)

    w3_wide[...] = jnp.zeros_like(w3_wide)
    load_w3.wait()
    last_layer = w3_narrow[...].astype(F32)
    for j in range(PACK):
        w3_wide[j * SLOT:j * SLOT + horizon, :] = last_layer
    w3[...] = w3_wide[...].T.astype(BF16)

    pl.semaphore_wait(barrier, n_dept + n_store - 2)

    def send_store(off):
        return pltpu.make_async_remote_copy(
            src_ref=store_sums.at[dept_at(off)], dst_ref=store_recv.at[off],
            send_sem=ss_send.at[off], recv_sem=ss_get.at[off],
            device_id=(my_store, dept_at(off)), device_id_type=MESH,
        )

    def send_item(off):
        return pltpu.make_async_remote_copy(
            src_ref=item_sums.at[store_at(off)], dst_ref=item_recv.at[off],
            send_sem=is_send.at[off], recv_sem=is_get.at[off],
            device_id=(store_at(off), my_dept), device_id_type=MESH,
        )

    item_total = None
    for off in dept_order:
        load_chunk(off).wait()
        sums = jnp.dot(selector[...], hist[rows_of(dept_at(off)), :], preferred_element_type=F32)
        store_sums[dept_at(off)] = sums[:own]
        if off:
            send_store(off).start()
        item_total = sums[own:] if item_total is None else item_total + sums[own:]
    item_acc[...] = jnp.zeros_like(item_acc)
    item_acc[0:items, :] = item_total
    for place in range(n_store):
        item_sums[place] = item_acc[place * item_share:(place + 1) * item_share, :]
    for off in range(1, n_store):
        send_item(off).start()

    load_w1.wait()
    load_w2.wait()
    half = 128
    lane = lax.broadcasted_iota(jnp.int32, (half, 128), 1)
    col_parts = [None] * groups

    def send_cs(off, part):
        return pltpu.make_async_remote_copy(
            src_ref=cs.at[part], dst_ref=cs_recv.at[off, part],
            send_sem=cs_send.at[off, part], recv_sem=cs_get.at[off, part],
            device_id=(my_store, dept_at(off)), device_id_type=MESH,
        )

    def send_up(off):
        return pltpu.make_async_remote_copy(
            src_ref=up, dst_ref=up_recv.at[off], send_sem=up_send.at[off], recv_sem=up_get.at[off],
            device_id=(my_store, dept_at(off)), device_id_type=MESH,
        )

    def scale(first, count):
        for start in range(first, first + count, SCALED_ROWS):
            rows = slice(start, start + SCALED_ROWS)
            root_mean = scales(hist[rows, :].astype(F32))
            flat[rows, :] = jnp.broadcast_to(root_mean, (SCALED_ROWS, 128))
            scaled[rows, :] = (hist[rows, :].astype(F32) * (1.0 / root_mean)).astype(BF16)

    def run(first, sizes, more=()):
        starts = [first + sum(sizes[:i]) for i in range(len(sizes))]
        pieces = [slice(start, start + size) for start, size in zip(starts, sizes)]
        results = layers(list(more) + [scaled[rows, :] for rows in pieces], w1, w2, w3)
        for rows, result in zip(pieces, results[len(more):]):
            flat[rows, :] = result * flat[rows, :]
        return results[:len(more)]

    def turn(part):
        row_part = None
        for k in range(groups):
            mixed = jnp.zeros((half, 128), F32)
            for j in range(PACK):
                if k * PACK + j < items:
                    one = flat[pl.ds(part * half * items + k * PACK + j, half, stride=items), :]
                    mixed = jnp.where((lane >= j * SLOT) & (lane < (j + 1) * SLOT), one, mixed)
            col_sum = jnp.sum(mixed, axis=0, keepdims=True)
            col_parts[k] = col_sum if col_parts[k] is None else col_parts[k] + col_sum
            turned = mixed.T
            base[k * 128:(k + 1) * 128, part * half:(part + 1) * half] = turned
            row_part = turned if row_part is None else row_part + turned
        cs[part] = sum(row_part[j * SLOT:(j + 1) * SLOT] for j in range(PACK))
        for off in dept_order[:-1]:
            send_cs(off, part).start()

    block = STORES_IN_CHUNK * items
    blocks = stores // STORES_IN_CHUNK
    blocks_in_half = half // STORES_IN_CHUNK
    scale(0, 2 * block)
    for number in range(0, blocks - 2, 2):
        run(number * block, [block, block])
        scale((number + 2) * block, 2 * block)
        if (number + 2) % blocks_in_half == 0:
            turn((number + 2) // blocks_in_half - 1)

    sum_rows[own:, :] = jnp.zeros((sum_rows.shape[0] - own, days), F32)
    store_total = store_sums[my_dept]
    for off in range(1, n_dept):
        send_store(off).wait_recv()
        store_total = store_total + store_recv[off]
    sum_rows[0:own, :] = store_total
    item_total = item_sums[my_store]
    for off in range(1, n_store):
        send_item(off).wait_recv()
        item_total = item_total + item_recv[off]
    sum_rows[own:own + item_share, :] = item_total
    upper_mean = scales(sum_rows[...])
    upper_scaled = (sum_rows[...] * (1.0 / upper_mean)).astype(BF16)
    (upper,) = run((blocks - 2) * block, [block], [upper_scaled])
    upper = upper * upper_mean
    up[...] = jnp.concatenate([upper[:own]] * (128 // own), axis=0).T[:SLOT]
    for off in dept_order[:-1]:
        send_up(off).start()

    run((blocks - 1) * block, [block // 2, block // 2])
    turn(stores // half - 1)
    write_base = pltpu.make_async_copy(base, base_out, out_sem.at[0])
    write_base.start()

    packed = lax.broadcasted_iota(jnp.int32, ci.shape, 0) * PACK
    packed_lane = lax.broadcasted_iota(jnp.int32, ci.shape, 1)
    for j in range(1, PACK):
        packed = packed + (packed_lane >= j * SLOT).astype(jnp.int32)
    ci[...] = jnp.zeros_like(ci)
    for k in range(groups):
        ci[k:k + 1, :] = 0.0 - col_parts[k]
    ci_mine = ci[...]
    for t in range(item_share):
        number = my_store * item_share + t
        ci_mine = ci_mine + jnp.where((packed == number) & (packed < items), upper[own + t:own + t + 1], 0.0)
    base_total = sum(col_parts)
    base_total = base_total + pltpu.roll(base_total, 2 * SLOT, 1)
    base_total = base_total + pltpu.roll(base_total, SLOT, 1)
    ci[...] = ci_mine
    ci[groups:groups + 1, :] = jnp.sum(upper[:own], axis=0, keepdims=True) - base_total
    ci[groups + 1:groups + 2, :] = jnp.sum(upper[own:own + item_share], axis=0, keepdims=True) - base_total

    def send_ci(off):
        return pltpu.make_async_remote_copy(
            src_ref=ci, dst_ref=ci_recv.at[off], send_sem=ci_send.at[off], recv_sem=ci_get.at[off],
            device_id=(store_at(off), my_dept), device_id_type=MESH,
        )

    def send_err(off):
        return pltpu.make_async_remote_copy(
            src_ref=err, dst_ref=err_recv.at[off], send_sem=err_send.at[off], recv_sem=err_get.at[off],
            device_id=(my_store, dept_at(off)), device_id_type=MESH,
        )

    for off in range(1, n_store):
        send_ci(off).start()

    item_err = ci[...]
    for off in range(1, n_store):
        send_ci(off).wait_recv()
        item_err = item_err + ci_recv[off]

    err[...] = item_err[groups:groups + 2]
    for off in range(1, n_dept):
        send_err(off).start()

    place = lax.broadcasted_iota(jnp.int32, (SLOT, stores), 1)

    def placed(piece, owner):
        mine = (place >= owner * own) & (place < (owner + 1) * own)
        return jnp.where(mine, jnp.concatenate([piece] * (stores // 128), axis=1), 0.0)

    store_parts = [cs[part] for part in range(stores // half)]
    store_err = placed(up[...], my_dept)
    for off in range(1, n_dept):
        for part in range(stores // half):
            send_cs(off, part).wait_recv()
            store_parts[part] = store_parts[part] + cs_recv[off, part]
        send_up(off).wait_recv()
        store_err = store_err + placed(up_recv[off], dept_at(n_dept - off))
    store_err = store_err - jnp.concatenate(store_parts, axis=1)
    errs = err[...]
    for off in range(1, n_dept):
        send_err(off).wait_recv()
        errs = errs + err_recv[off]
    err_s, err_i = errs[0:1], errs[1:2]
    item_count = float(items * n_dept)
    store_count = float(stores * n_store)
    denominator = 1.0 + item_count + store_count
    shift_s = (err_s * (1.0 + store_count) - store_count * err_i) / denominator
    shift_i = ((1.0 + item_count) * err_i - item_count * err_s) / denominator
    shift_i_col = jnp.broadcast_to(shift_i, (128, 128)).T[:SLOT]
    shift_i_all = jnp.concatenate([shift_i_col] * (stores // 128), axis=1)
    small[0:SLOT, :] = (store_err - shift_i_all) * (1.0 / (1.0 + item_count))
    small[SLOT:2 * SLOT, :] = store_err * (1.0 / math.sqrt(item_count))
    small[2 * SLOT:, 0:128] = (item_err - shift_s) * (1.0 / (1.0 + store_count))
    small[2 * SLOT:, 128:256] = item_err * (1.0 / math.sqrt(store_count))
    write_small = pltpu.make_async_copy(small, small_out, out_sem.at[1])
    write_small.start()

    for off in range(1, n_dept):
        send_store(off).wait_send()
        send_up(off).wait_send()
        send_err(off).wait_send()
        for part in range(stores // half):
            send_cs(off, part).wait_send()
    for off in range(1, n_store):
        send_item(off).wait_send()
        send_ci(off).wait_send()
    write_base.wait()
    write_small.wait()


def final_kernel(
    items, horizon, base_hbm, small_hbm, reconciled_out, store_gap_out, item_gap_out,
    base, small, reconciled, store_gap, item_gap, read_sem, write_sem,
):
    groups = base.shape[0] // 128
    read_small = pltpu.make_async_copy(small_hbm, small, read_sem.at[groups])
    read_small.start()
    reads, writes = [], []
    for k in range(groups):
        rows = pl.ds(k * 128, 128)
        reads.append(pltpu.make_async_copy(base_hbm.at[rows], base.at[rows], read_sem.at[k]))
        reads[k].start()
    read_small.wait()
    shift = small[0:SLOT, :]
    item_shift = small[2 * SLOT:, 0:128]
    gap = small[2 * SLOT:, 128:256]
    columns = jnp.concatenate([item_shift] + [jnp.zeros((128 - item_shift.shape[0], 128), F32)], axis=0).T
    store_gap[...] = small[SLOT:SLOT + horizon, :]
    for item in range(items):
        k, j = divmod(item, PACK)
        item_gap[item:item + 1, :] = gap[k:k + 1, j * SLOT:j * SLOT + horizon]
    writes.append(pltpu.make_async_copy(store_gap, store_gap_out, write_sem.at[groups]))
    writes.append(pltpu.make_async_copy(item_gap, item_gap_out, write_sem.at[groups + 1]))
    writes[0].start()
    writes[1].start()
    for k in range(groups):
        reads[k].wait()
        mine = range(k * PACK, min((k + 1) * PACK, items))
        for item in mine:
            j = item - k * PACK
            first = k * 128 + j * SLOT
            block = base[first:first + SLOT, :] + shift + columns[j * SLOT:(j + 1) * SLOT, k:k + 1]
            reconciled[item * horizon:(item + 1) * horizon, :] = block[:horizon]
        rows = pl.ds(mine[0] * horizon, len(mine) * horizon)
        writes.append(pltpu.make_async_copy(reconciled.at[rows], reconciled_out.at[rows], write_sem.at[k]))
        writes[-1].start()
    for write in writes:
        write.wait()


def body(n_store, n_dept, history, input_layer_matrix, middle_layer_matrix, final_layer_matrix):
    stores, items, days = history.shape
    hidden = input_layer_matrix.shape[1]
    horizon = final_layer_matrix.shape[1]
    own = stores // n_dept
    item_share = -(-items // n_store)
    groups = -(-items // PACK)
    group_rows = -(-(groups + 2) // 8) * 8
    share_rows = -(-item_share // 8) * 8
    in_hbm = pl.BlockSpec(memory_space=pl.ANY)
    dma = pltpu.SemaphoreType.DMA
    shape = jax.ShapeDtypeStruct
    parts = pl.pallas_call(
        functools.partial(main_kernel, n_store, n_dept, stores, items, horizon),
        out_shape=(
            shape((groups * 128, stores), F32),
            shape((2 * SLOT + group_rows, stores), F32),
        ),
        in_specs=[in_hbm] * 4,
        out_specs=[in_hbm] * 2,
        scratch_shapes=[
            pltpu.VMEM((groups * 128, stores), F32),
            pltpu.VMEM((2 * SLOT + group_rows, stores), F32),
            pltpu.VMEM((stores * items, days), BF16),
            pltpu.VMEM((stores * items, days), BF16),
            pltpu.VMEM((days, hidden), BF16),
            pltpu.VMEM((hidden, hidden), BF16),
            pltpu.VMEM((horizon, hidden), BF16),
            pltpu.VMEM((128, hidden), F32),
            pltpu.VMEM((hidden, 128), BF16),
            pltpu.VMEM((own + items, own * items), BF16),
            pltpu.VMEM((n_dept, own, days), F32),
            pltpu.VMEM((n_dept, own, days), F32),
            pltpu.VMEM((-(-n_store * item_share // 8) * 8, days), F32),
            pltpu.VMEM((n_store, item_share, days), F32),
            pltpu.VMEM((n_store, item_share, days), F32),
            pltpu.VMEM((own + share_rows, days), F32),
            pltpu.VMEM((stores * items, 128), F32),
            pltpu.VMEM((stores // 128, SLOT, 128), F32),
            pltpu.VMEM((n_dept, stores // 128, SLOT, 128), F32),
            pltpu.VMEM((SLOT, 128), F32),
            pltpu.VMEM((n_dept, SLOT, 128), F32),
            pltpu.VMEM((group_rows, 128), F32),
            pltpu.VMEM((n_store, group_rows, 128), F32),
            pltpu.VMEM((2, 128), F32),
            pltpu.VMEM((n_dept, 2, 128), F32),
            dma((n_dept,)),
            dma((3,)),
            dma((n_dept,)),
            dma((n_dept,)),
            dma((n_store,)),
            dma((n_store,)),
            dma((n_dept, stores // 128)),
            dma((n_dept, stores // 128)),
            dma((n_dept,)),
            dma((n_dept,)),
            dma((n_store,)),
            dma((n_store,)),
            dma((n_dept,)),
            dma((n_dept,)),
            dma((2,)),
        ],
        compiler_params=pltpu.CompilerParams(
            collective_id=0, has_side_effects=True, vmem_limit_bytes=60 * 2**20
        ),
    )(
        history.reshape(stores * items, days),
        input_layer_matrix,
        middle_layer_matrix,
        final_layer_matrix.T,
    )
    reconciled, store_gap, item_gap = pl.pallas_call(
        functools.partial(final_kernel, items, horizon),
        out_shape=(
            shape((items * horizon, stores), F32),
            shape((horizon, stores), F32),
            shape((items, horizon), F32),
        ),
        in_specs=[in_hbm] * 2,
        out_specs=[in_hbm] * 3,
        scratch_shapes=[
            pltpu.VMEM((groups * 128, stores), F32),
            pltpu.VMEM((2 * SLOT + group_rows, stores), F32),
            pltpu.VMEM((items * horizon, stores), F32),
            pltpu.VMEM((horizon, stores), F32),
            pltpu.VMEM((items, horizon), F32),
            dma((groups + 1,)),
            dma((groups + 2,)),
        ],
        compiler_params=pltpu.CompilerParams(vmem_limit_bytes=60 * 2**20),
    )(*parts)
    return reconciled.T, store_gap, item_gap.T


def solution(mesh):
    return jax.shard_map(
        functools.partial(body, mesh.shape["store"], mesh.shape["dept"]),
        mesh=mesh,
        in_specs=(P("store", "dept", None), P(), P(), P()),
        out_specs=(P("store", "dept"), P(None, "store"), P(None, "dept")),
        check_vma=False,
    )
```

```python
import functools
import math

import jax
import jax.numpy as jnp
from jax import lax
from jax.experimental import pallas as pl
from jax.experimental.pallas import tpu as pltpu
from jax.sharding import PartitionSpec as P

MESH = pl.DeviceIdType.MESH
F32 = jnp.float32
BF16 = jnp.bfloat16
SLOT = 32
PACK = 4
STORES_IN_CHUNK = 32
SCALED_ROWS = 128


def scales(values):
    mean = jnp.sum(values * values, axis=-1, keepdims=True) * (1.0 / values.shape[-1])
    return jnp.sqrt(mean + 1e-05)


def layers(blocks, w1, w2, w3):
    for weights in (w1, w2):
        blocks = [jnp.dot(block, weights[...], preferred_element_type=F32).astype(BF16) for block in blocks]
        blocks = [jnp.maximum(block, 0) for block in blocks]
    return [jnp.dot(block, w3[...], preferred_element_type=F32) for block in blocks]


def main_kernel(
    n_store, n_dept, stores, items, horizon,
    hist_hbm, w1_hbm, w2_hbm, w3_hbm,
    base_out, small_out,
    base, small, hist, scaled, w1, w2, w3_narrow, w3_wide, w3, selector, store_sums, pair_recv, store_recv, item_acc, item_sums, item_recv,
    sum_rows, flat, cs, cs_recv, up, up_recv, ci, ci_recv, err, err_recv,
    hist_sem, weight_sem, sp_send, sp_get, ss_send, ss_get, is_send, is_get, cs_send, cs_get, up_send, up_get,
    ci_send, ci_get, err_send, err_get, out_sem,
):
    my_store = lax.axis_index("store")
    my_dept = lax.axis_index("dept")
    own = stores // n_dept
    own_rows = own * items
    days = hist.shape[1]
    item_share = item_sums.shape[1]
    groups = -(-items // PACK)
    dept_order = sorted(range(1, n_dept), key=lambda o: -min(o, n_dept - o)) + [0]

    def dept_at(off):
        return lax.rem(my_dept + off, n_dept)

    def store_at(off):
        return lax.rem(my_store + off, n_store)

    def rows_of(chunk):
        return pl.ds(pl.multiple_of(chunk * own_rows, own_rows), own_rows)

    def load_chunk(slot, chunk):
        rows = rows_of(chunk)
        return pltpu.make_async_copy(hist_hbm.at[rows], hist.at[rows], hist_sem.at[slot])

    early = lax.rem(my_dept + 1, 2) + my_dept - lax.rem(my_dept, 2)
    for slot in range(n_dept):
        near = slot % (n_dept // 2) == n_dept // 2 - 1
        ahead = 0 if near else 2 * (slot % (n_dept // 2) + 1)
        load_chunk(slot, lax.rem((early if slot < n_dept // 2 else my_dept) + ahead, n_dept)).start()
    load_w1 = pltpu.make_async_copy(w1_hbm, w1, weight_sem.at[0])
    load_w2 = pltpu.make_async_copy(w2_hbm, w2, weight_sem.at[1])
    load_w3 = pltpu.make_async_copy(w3_hbm, w3_narrow, weight_sem.at[2])
    load_w3.start()
    load_w1.start()
    load_w2.start()

    barrier = pltpu.get_barrier_semaphore()

    for off in range(1, n_dept):
        pl.semaphore_signal(barrier, inc=1, device_id=(my_store, dept_at(off)), device_id_type=MESH)
    for off in range(1, n_store):
        pl.semaphore_signal(barrier, inc=1, device_id=(store_at(off), my_dept), device_id_type=MESH)

    row = lax.broadcasted_iota(jnp.int32, selector.shape, 0)
    col = lax.broadcasted_iota(jnp.int32, selector.shape, 1)
    of_store = (col >= row * items) & (col < row * items + items)
    col_f = col.astype(F32)
    which = col_f - items * jnp.floor((col_f + 0.5) * (1.0 / items))
    of_item = which == (row - own).astype(F32)
    selector[...] = jnp.where(row < own, of_store.astype(F32), of_item.astype(F32)).astype(BF16)

    w3_wide[...] = jnp.zeros_like(w3_wide)
    load_w3.wait()
    last_layer = w3_narrow[...].astype(F32)
    for j in range(PACK):
        w3_wide[j * SLOT:j * SLOT + horizon, :] = last_layer
    w3[...] = w3_wide[...].T.astype(BF16)

    pl.semaphore_wait(barrier, n_dept + n_store - 2)

    partner = my_dept + 1 - 2 * lax.rem(my_dept, 2)
    pairs = n_dept // 2

    def partner_block(m):
        return lax.rem(partner + 2 * m, n_dept)

    def send_pair(m):
        return pltpu.make_async_remote_copy(
            src_ref=store_sums.at[partner_block(m)], dst_ref=pair_recv.at[m],
            send_sem=sp_send.at[m], recv_sem=sp_get.at[m],
            device_id=(my_store, partner), device_id_type=MESH,
        )

    def send_store(m):
        return pltpu.make_async_remote_copy(
            src_ref=store_sums.at[dept_at(2 * m)], dst_ref=store_recv.at[m],
            send_sem=ss_send.at[m], recv_sem=ss_get.at[m],
            device_id=(my_store, dept_at(2 * m)), device_id_type=MESH,
        )

    def send_item(off):
        return pltpu.make_async_remote_copy(
            src_ref=item_sums.at[store_at(off)], dst_ref=item_recv.at[off],
            send_sem=is_send.at[off], recv_sem=is_get.at[off],
            device_id=(store_at(off), my_dept), device_id_type=MESH,
        )

    item_total = None
    far_first = list(range(1, pairs)) + [0]
    for slot, (m, sent) in enumerate([(m, True) for m in far_first] + [(m, False) for m in far_first]):
        chunk = partner_block(m) if sent else dept_at(2 * m)
        load_chunk(slot, chunk).wait()
        sums = jnp.dot(selector[...], hist[rows_of(chunk), :], preferred_element_type=F32)
        store_sums[chunk] = sums[:own]
        if sent:
            send_pair(m).start()
        item_total = sums[own:] if item_total is None else item_total + sums[own:]
    item_acc[...] = jnp.zeros_like(item_acc)
    item_acc[0:items, :] = item_total
    for place in range(n_store):
        item_sums[place] = item_acc[place * item_share:(place + 1) * item_share, :]
    for off in range(1, n_store):
        send_item(off).start()

    load_w1.wait()
    load_w2.wait()
    half = 128
    lane = lax.broadcasted_iota(jnp.int32, (half, 128), 1)
    col_parts = [None] * groups

    def send_cs(off, part):
        return pltpu.make_async_remote_copy(
            src_ref=cs.at[part], dst_ref=cs_recv.at[off, part],
            send_sem=cs_send.at[off, part], recv_sem=cs_get.at[off, part],
            device_id=(my_store, dept_at(off)), device_id_type=MESH,
        )

    def send_up(off):
        return pltpu.make_async_remote_copy(
            src_ref=up, dst_ref=up_recv.at[off], send_sem=up_send.at[off], recv_sem=up_get.at[off],
            device_id=(my_store, dept_at(off)), device_id_type=MESH,
        )

    def scale(first, count):
        for start in range(first, first + count, SCALED_ROWS):
            rows = slice(start, start + SCALED_ROWS)
            root_mean = scales(hist[rows, :].astype(F32))
            flat[rows, :] = jnp.broadcast_to(root_mean, (SCALED_ROWS, 128))
            scaled[rows, :] = (hist[rows, :].astype(F32) * (1.0 / root_mean)).astype(BF16)

    def run(first, sizes, more=()):
        starts = [first + sum(sizes[:i]) for i in range(len(sizes))]
        pieces = [slice(start, start + size) for start, size in zip(starts, sizes)]
        results = layers(list(more) + [scaled[rows, :] for rows in pieces], w1, w2, w3)
        for rows, result in zip(pieces, results[len(more):]):
            flat[rows, :] = result * flat[rows, :]
        return results[:len(more)]

    def turn(part):
        row_part = None
        for k in range(groups):
            mixed = jnp.zeros((half, 128), F32)
            for j in range(PACK):
                if k * PACK + j < items:
                    one = flat[pl.ds(part * half * items + k * PACK + j, half, stride=items), :]
                    mixed = jnp.where((lane >= j * SLOT) & (lane < (j + 1) * SLOT), one, mixed)
            col_sum = jnp.sum(mixed, axis=0, keepdims=True)
            col_parts[k] = col_sum if col_parts[k] is None else col_parts[k] + col_sum
            turned = mixed.T
            base[k * 128:(k + 1) * 128, part * half:(part + 1) * half] = turned
            row_part = turned if row_part is None else row_part + turned
        cs[part] = sum(row_part[j * SLOT:(j + 1) * SLOT] for j in range(PACK))
        for off in dept_order[:-1]:
            send_cs(off, part).start()

    block = STORES_IN_CHUNK * items
    blocks = stores // STORES_IN_CHUNK
    blocks_in_half = half // STORES_IN_CHUNK
    scale(0, 2 * block)
    for number in range(0, blocks - 2, 2):
        run(number * block, [block, block])
        scale((number + 2) * block, 2 * block)
        if number == 0:
            for m in range(1, pairs):
                send_pair(m).wait_recv()
                store_sums[dept_at(2 * m)] = store_sums[dept_at(2 * m)] + pair_recv[m]
                send_store(m).start()
        if (number + 2) % blocks_in_half == 0:
            turn((number + 2) // blocks_in_half - 1)

    run((blocks - 2) * block, [block // 2, block // 2])

    sum_rows[own:, :] = jnp.zeros((sum_rows.shape[0] - own, days), F32)
    send_pair(0).wait_recv()
    store_total = store_sums[my_dept] + pair_recv[0]
    for m in range(1, pairs):
        send_store(m).wait_recv()
        store_total = store_total + store_recv[m]
    sum_rows[0:own, :] = store_total
    item_total = item_sums[my_store]
    for off in range(1, n_store):
        send_item(off).wait_recv()
        item_total = item_total + item_recv[off]
    sum_rows[own:own + item_share, :] = item_total
    upper_mean = scales(sum_rows[...])
    upper_scaled = (sum_rows[...] * (1.0 / upper_mean)).astype(BF16)
    (upper,) = run((blocks - 1) * block, [block], [upper_scaled])
    upper = upper * upper_mean
    up[...] = jnp.concatenate([upper[:own]] * (128 // own), axis=0).T[:SLOT]
    for off in dept_order[:-1]:
        send_up(off).start()

    turn(stores // half - 1)
    write_base = pltpu.make_async_copy(base, base_out, out_sem.at[0])
    write_base.start()

    packed = lax.broadcasted_iota(jnp.int32, ci.shape, 0) * PACK
    packed_lane = lax.broadcasted_iota(jnp.int32, ci.shape, 1)
    for j in range(1, PACK):
        packed = packed + (packed_lane >= j * SLOT).astype(jnp.int32)
    ci[...] = jnp.zeros_like(ci)
    for k in range(groups):
        ci[k:k + 1, :] = 0.0 - col_parts[k]
    ci_mine = ci[...]
    for t in range(item_share):
        number = my_store * item_share + t
        ci_mine = ci_mine + jnp.where((packed == number) & (packed < items), upper[own + t:own + t + 1], 0.0)
    base_total = sum(col_parts)
    base_total = base_total + pltpu.roll(base_total, 2 * SLOT, 1)
    base_total = base_total + pltpu.roll(base_total, SLOT, 1)
    ci[...] = ci_mine
    ci[groups:groups + 1, :] = jnp.sum(upper[:own], axis=0, keepdims=True) - base_total
    ci[groups + 1:groups + 2, :] = jnp.sum(upper[own:own + item_share], axis=0, keepdims=True) - base_total

    def send_ci(off):
        return pltpu.make_async_remote_copy(
            src_ref=ci, dst_ref=ci_recv.at[off], send_sem=ci_send.at[off], recv_sem=ci_get.at[off],
            device_id=(store_at(off), my_dept), device_id_type=MESH,
        )

    def send_err(off):
        return pltpu.make_async_remote_copy(
            src_ref=err, dst_ref=err_recv.at[off], send_sem=err_send.at[off], recv_sem=err_get.at[off],
            device_id=(my_store, dept_at(off)), device_id_type=MESH,
        )

    for off in range(1, n_store):
        send_ci(off).start()

    item_err = ci[...]
    for off in range(1, n_store):
        send_ci(off).wait_recv()
        item_err = item_err + ci_recv[off]

    err[...] = item_err[groups:groups + 2]
    for off in range(1, n_dept):
        send_err(off).start()

    place = lax.broadcasted_iota(jnp.int32, (SLOT, stores), 1)

    def placed(piece, owner):
        mine = (place >= owner * own) & (place < (owner + 1) * own)
        return jnp.where(mine, jnp.concatenate([piece] * (stores // 128), axis=1), 0.0)

    store_parts = [cs[part] for part in range(stores // half)]
    store_err = placed(up[...], my_dept)
    for off in range(1, n_dept):
        for part in range(stores // half):
            send_cs(off, part).wait_recv()
            store_parts[part] = store_parts[part] + cs_recv[off, part]
        send_up(off).wait_recv()
        store_err = store_err + placed(up_recv[off], dept_at(n_dept - off))
    store_err = store_err - jnp.concatenate(store_parts, axis=1)
    errs = err[...]
    for off in range(1, n_dept):
        send_err(off).wait_recv()
        errs = errs + err_recv[off]
    err_s, err_i = errs[0:1], errs[1:2]
    item_count = float(items * n_dept)
    store_count = float(stores * n_store)
    denominator = 1.0 + item_count + store_count
    shift_s = (err_s * (1.0 + store_count) - store_count * err_i) / denominator
    shift_i = ((1.0 + item_count) * err_i - item_count * err_s) / denominator
    shift_i_col = jnp.broadcast_to(shift_i, (128, 128)).T[:SLOT]
    shift_i_all = jnp.concatenate([shift_i_col] * (stores // 128), axis=1)
    small[0:SLOT, :] = (store_err - shift_i_all) * (1.0 / (1.0 + item_count))
    small[SLOT:2 * SLOT, :] = store_err * (1.0 / math.sqrt(item_count))
    small[2 * SLOT:, 0:128] = (item_err - shift_s) * (1.0 / (1.0 + store_count))
    small[2 * SLOT:, 128:256] = item_err * (1.0 / math.sqrt(store_count))
    write_small = pltpu.make_async_copy(small, small_out, out_sem.at[1])
    write_small.start()

    for off in range(1, n_dept):
        send_up(off).wait_send()
        send_err(off).wait_send()
        for part in range(stores // half):
            send_cs(off, part).wait_send()
    for m in range(pairs):
        send_pair(m).wait_send()
        if m:
            send_store(m).wait_send()
    for off in range(1, n_store):
        send_item(off).wait_send()
        send_ci(off).wait_send()
    write_base.wait()
    write_small.wait()


def final_kernel(
    items, horizon, base_hbm, small_hbm, reconciled_out, store_gap_out, item_gap_out,
    base, small, reconciled, store_gap, item_gap, read_sem, write_sem,
):
    groups = base.shape[0] // 128
    read_small = pltpu.make_async_copy(small_hbm, small, read_sem.at[groups])
    read_small.start()
    reads, writes = [], []
    for k in range(groups):
        rows = pl.ds(k * 128, 128)
        reads.append(pltpu.make_async_copy(base_hbm.at[rows], base.at[rows], read_sem.at[k]))
        reads[k].start()
    read_small.wait()
    shift = small[0:SLOT, :]
    item_shift = small[2 * SLOT:, 0:128]
    gap = small[2 * SLOT:, 128:256]
    columns = jnp.concatenate([item_shift] + [jnp.zeros((128 - item_shift.shape[0], 128), F32)], axis=0).T
    store_gap[...] = small[SLOT:SLOT + horizon, :]
    for item in range(items):
        k, j = divmod(item, PACK)
        item_gap[item:item + 1, :] = gap[k:k + 1, j * SLOT:j * SLOT + horizon]
    writes.append(pltpu.make_async_copy(store_gap, store_gap_out, write_sem.at[groups]))
    writes.append(pltpu.make_async_copy(item_gap, item_gap_out, write_sem.at[groups + 1]))
    writes[0].start()
    writes[1].start()
    for k in range(groups):
        reads[k].wait()
        mine = range(k * PACK, min((k + 1) * PACK, items))
        for item in mine:
            j = item - k * PACK
            first = k * 128 + j * SLOT
            block = base[first:first + SLOT, :] + shift + columns[j * SLOT:(j + 1) * SLOT, k:k + 1]
            reconciled[item * horizon:(item + 1) * horizon, :] = block[:horizon]
        rows = pl.ds(mine[0] * horizon, len(mine) * horizon)
        writes.append(pltpu.make_async_copy(reconciled.at[rows], reconciled_out.at[rows], write_sem.at[k]))
        writes[-1].start()
    for write in writes:
        write.wait()


def body(n_store, n_dept, history, input_layer_matrix, middle_layer_matrix, final_layer_matrix):
    stores, items, days = history.shape
    hidden = input_layer_matrix.shape[1]
    horizon = final_layer_matrix.shape[1]
    own = stores // n_dept
    item_share = -(-items // n_store)
    groups = -(-items // PACK)
    group_rows = -(-(groups + 2) // 8) * 8
    share_rows = -(-item_share // 8) * 8
    in_hbm = pl.BlockSpec(memory_space=pl.ANY)
    dma = pltpu.SemaphoreType.DMA
    shape = jax.ShapeDtypeStruct
    parts = pl.pallas_call(
        functools.partial(main_kernel, n_store, n_dept, stores, items, horizon),
        out_shape=(
            shape((groups * 128, stores), F32),
            shape((2 * SLOT + group_rows, stores), F32),
        ),
        in_specs=[in_hbm] * 4,
        out_specs=[in_hbm] * 2,
        scratch_shapes=[
            pltpu.VMEM((groups * 128, stores), F32),
            pltpu.VMEM((2 * SLOT + group_rows, stores), F32),
            pltpu.VMEM((stores * items, days), BF16),
            pltpu.VMEM((stores * items, days), BF16),
            pltpu.VMEM((days, hidden), BF16),
            pltpu.VMEM((hidden, hidden), BF16),
            pltpu.VMEM((horizon, hidden), BF16),
            pltpu.VMEM((128, hidden), F32),
            pltpu.VMEM((hidden, 128), BF16),
            pltpu.VMEM((own + items, own * items), BF16),
            pltpu.VMEM((n_dept, own, days), F32),
            pltpu.VMEM((n_dept // 2, own, days), F32),
            pltpu.VMEM((n_dept // 2, own, days), F32),
            pltpu.VMEM((-(-n_store * item_share // 8) * 8, days), F32),
            pltpu.VMEM((n_store, item_share, days), F32),
            pltpu.VMEM((n_store, item_share, days), F32),
            pltpu.VMEM((own + share_rows, days), F32),
            pltpu.VMEM((stores * items, 128), F32),
            pltpu.VMEM((stores // 128, SLOT, 128), F32),
            pltpu.VMEM((n_dept, stores // 128, SLOT, 128), F32),
            pltpu.VMEM((SLOT, 128), F32),
            pltpu.VMEM((n_dept, SLOT, 128), F32),
            pltpu.VMEM((group_rows, 128), F32),
            pltpu.VMEM((n_store, group_rows, 128), F32),
            pltpu.VMEM((2, 128), F32),
            pltpu.VMEM((n_dept, 2, 128), F32),
            dma((n_dept,)),
            dma((3,)),
            dma((n_dept // 2,)),
            dma((n_dept // 2,)),
            dma((n_dept // 2,)),
            dma((n_dept // 2,)),
            dma((n_store,)),
            dma((n_store,)),
            dma((n_dept, stores // 128)),
            dma((n_dept, stores // 128)),
            dma((n_dept,)),
            dma((n_dept,)),
            dma((n_store,)),
            dma((n_store,)),
            dma((n_dept,)),
            dma((n_dept,)),
            dma((2,)),
        ],
        compiler_params=pltpu.CompilerParams(
            collective_id=0, has_side_effects=True, vmem_limit_bytes=60 * 2**20
        ),
    )(
        history.reshape(stores * items, days),
        input_layer_matrix,
        middle_layer_matrix,
        final_layer_matrix.T,
    )
    reconciled, store_gap, item_gap = pl.pallas_call(
        functools.partial(final_kernel, items, horizon),
        out_shape=(
            shape((items * horizon, stores), F32),
            shape((horizon, stores), F32),
            shape((items, horizon), F32),
        ),
        in_specs=[in_hbm] * 2,
        out_specs=[in_hbm] * 3,
        scratch_shapes=[
            pltpu.VMEM((groups * 128, stores), F32),
            pltpu.VMEM((2 * SLOT + group_rows, stores), F32),
            pltpu.VMEM((items * horizon, stores), F32),
            pltpu.VMEM((horizon, stores), F32),
            pltpu.VMEM((items, horizon), F32),
            dma((groups + 1,)),
            dma((groups + 2,)),
        ],
        compiler_params=pltpu.CompilerParams(vmem_limit_bytes=60 * 2**20),
    )(*parts)
    return reconciled.T, store_gap, item_gap.T


def solution(mesh):
    return jax.shard_map(
        functools.partial(body, mesh.shape["store"], mesh.shape["dept"]),
        mesh=mesh,
        in_specs=(P("store", "dept", None), P(), P(), P()),
        out_specs=(P("store", "dept"), P(None, "store"), P(None, "dept")),
        check_vma=False,
    )
```

```python
import functools
import math

import jax
import jax.numpy as jnp
from jax import lax
from jax.experimental import pallas as pl
from jax.experimental.pallas import tpu as pltpu
from jax.sharding import PartitionSpec as P

MESH = pl.DeviceIdType.MESH
F32 = jnp.float32
BF16 = jnp.bfloat16
SLOT = 32
PACK = 4
STORES_IN_CHUNK = 32
SCALED_ROWS = 128


def scales(values):
    mean = jnp.sum(values * values, axis=-1, keepdims=True) * (1.0 / values.shape[-1])
    return jnp.sqrt(mean + 1e-05)


def layers(blocks, w1, w2, w3):
    for weights in (w1, w2):
        blocks = [jnp.dot(block, weights[...], preferred_element_type=F32).astype(BF16) for block in blocks]
        blocks = [jnp.maximum(block, 0) for block in blocks]
    return [jnp.dot(block, w3[...], preferred_element_type=F32) for block in blocks]


def main_kernel(
    n_store, n_dept, stores, items, horizon,
    hist_hbm, w1_hbm, w2_hbm, w3_hbm,
    base_out, small_out,
    base, small, hist, scaled, w1, w2, w3_narrow, w3_wide, w3, selector, store_sums, pair_recv, store_recv, item_acc, item_sums, item_recv,
    sum_rows, flat, cs, cs_recv, up, up_recv, ci, ci_recv, err, err_recv,
    hist_sem, weight_sem, sp_send, sp_get, ss_send, ss_get, is_send, is_get, cs_send, cs_get, up_send, up_get,
    ci_send, ci_get, err_send, err_get, out_sem,
):
    my_store = lax.axis_index("store")
    my_dept = lax.axis_index("dept")
    own = stores // n_dept
    own_rows = own * items
    days = hist.shape[1]
    item_share = item_sums.shape[1]
    groups = -(-items // PACK)
    dept_order = sorted(range(1, n_dept), key=lambda o: -min(o, n_dept - o)) + [0]

    def dept_at(off):
        return lax.rem(my_dept + off, n_dept)

    def store_at(off):
        return lax.rem(my_store + off, n_store)

    def rows_of(chunk):
        return pl.ds(pl.multiple_of(chunk * own_rows, own_rows), own_rows)

    def load_chunk(slot, chunk):
        rows = rows_of(chunk)
        return pltpu.make_async_copy(hist_hbm.at[rows], hist.at[rows], hist_sem.at[slot])

    early = lax.rem(my_dept + 1, 2) + my_dept - lax.rem(my_dept, 2)
    for slot in range(n_dept):
        near = slot % (n_dept // 2) == n_dept // 2 - 1
        ahead = 0 if near else 2 * (slot % (n_dept // 2) + 1)
        load_chunk(slot, lax.rem((early if slot < n_dept // 2 else my_dept) + ahead, n_dept)).start()
    load_w1 = pltpu.make_async_copy(w1_hbm, w1, weight_sem.at[0])
    load_w2 = pltpu.make_async_copy(w2_hbm, w2, weight_sem.at[1])
    load_w3 = pltpu.make_async_copy(w3_hbm, w3_narrow, weight_sem.at[2])
    load_w3.start()
    load_w1.start()
    load_w2.start()

    barrier = pltpu.get_barrier_semaphore()

    for off in range(1, n_dept):
        pl.semaphore_signal(barrier, inc=1, device_id=(my_store, dept_at(off)), device_id_type=MESH)
    for off in range(1, n_store):
        pl.semaphore_signal(barrier, inc=1, device_id=(store_at(off), my_dept), device_id_type=MESH)

    row = lax.broadcasted_iota(jnp.int32, selector.shape, 0)
    col = lax.broadcasted_iota(jnp.int32, selector.shape, 1)
    of_store = (col >= row * items) & (col < row * items + items)
    col_f = col.astype(F32)
    which = col_f - items * jnp.floor((col_f + 0.5) * (1.0 / items))
    of_item = which == (row - own).astype(F32)
    selector[...] = jnp.where(row < own, of_store.astype(F32), of_item.astype(F32)).astype(BF16)

    w3_wide[...] = jnp.zeros_like(w3_wide)
    load_w3.wait()
    last_layer = w3_narrow[...].astype(F32)
    for j in range(PACK):
        w3_wide[j * SLOT:j * SLOT + horizon, :] = last_layer
    w3[...] = w3_wide[...].T.astype(BF16)

    pl.semaphore_wait(barrier, n_dept + n_store - 2)

    partner = my_dept + 1 - 2 * lax.rem(my_dept, 2)
    pairs = n_dept // 2

    def partner_block(m):
        return lax.rem(partner + 2 * m, n_dept)

    def send_pair(m):
        return pltpu.make_async_remote_copy(
            src_ref=store_sums.at[partner_block(m)], dst_ref=pair_recv.at[m],
            send_sem=sp_send.at[m], recv_sem=sp_get.at[m],
            device_id=(my_store, partner), device_id_type=MESH,
        )

    def send_store(m):
        return pltpu.make_async_remote_copy(
            src_ref=store_sums.at[dept_at(2 * m)], dst_ref=store_recv.at[m],
            send_sem=ss_send.at[m], recv_sem=ss_get.at[m],
            device_id=(my_store, dept_at(2 * m)), device_id_type=MESH,
        )

    def send_item(off):
        return pltpu.make_async_remote_copy(
            src_ref=item_sums.at[store_at(off)], dst_ref=item_recv.at[off],
            send_sem=is_send.at[off], recv_sem=is_get.at[off],
            device_id=(store_at(off), my_dept), device_id_type=MESH,
        )

    item_total = None
    far_first = list(range(1, pairs)) + [0]
    for slot, (m, sent) in enumerate([(m, True) for m in far_first] + [(m, False) for m in far_first]):
        chunk = partner_block(m) if sent else dept_at(2 * m)
        load_chunk(slot, chunk).wait()
        sums = jnp.dot(selector[...], hist[rows_of(chunk), :], preferred_element_type=F32)
        store_sums[chunk] = sums[:own]
        if sent:
            send_pair(m).start()
        item_total = sums[own:] if item_total is None else item_total + sums[own:]
    item_acc[...] = jnp.zeros_like(item_acc)
    item_acc[0:items, :] = item_total
    for place in range(n_store):
        item_sums[place] = item_acc[place * item_share:(place + 1) * item_share, :]
    for off in range(1, n_store):
        send_item(off).start()

    load_w1.wait()
    load_w2.wait()
    half = 128
    lane = lax.broadcasted_iota(jnp.int32, (half, 128), 1)
    col_parts = [None] * groups

    def send_cs(off, part):
        return pltpu.make_async_remote_copy(
            src_ref=cs.at[part], dst_ref=cs_recv.at[off, part],
            send_sem=cs_send.at[off, part], recv_sem=cs_get.at[off, part],
            device_id=(my_store, dept_at(off)), device_id_type=MESH,
        )

    def send_up(off):
        return pltpu.make_async_remote_copy(
            src_ref=up, dst_ref=up_recv.at[off], send_sem=up_send.at[off], recv_sem=up_get.at[off],
            device_id=(my_store, dept_at(off)), device_id_type=MESH,
        )

    def scale(first, count):
        def step(i, carry):
            for part in range(3):
                start = first + (i * 3 + part) * SCALED_ROWS
                rows = pl.ds(pl.multiple_of(start, SCALED_ROWS), SCALED_ROWS)
                root_mean = scales(hist[rows, :].astype(F32))
                flat[rows, :] = jnp.broadcast_to(root_mean, (SCALED_ROWS, 128))
                scaled[rows, :] = (hist[rows, :].astype(F32) * (1.0 / root_mean)).astype(BF16)
            return carry

        lax.fori_loop(0, count // (3 * SCALED_ROWS), step, 0)

    def run(first, sizes, more=()):
        starts = [first + sum(sizes[:i]) for i in range(len(sizes))]
        pieces = [slice(start, start + size) for start, size in zip(starts, sizes)]
        results = layers(list(more) + [scaled[rows, :] for rows in pieces], w1, w2, w3)
        for rows, result in zip(pieces, results[len(more):]):
            flat[rows, :] = result * flat[rows, :]
        return results[:len(more)]

    def turn(part):
        row_part = None
        for k in range(groups):
            mixed = jnp.zeros((half, 128), F32)
            for j in range(PACK):
                if k * PACK + j < items:
                    one = flat[pl.ds(part * half * items + k * PACK + j, half, stride=items), :]
                    mixed = jnp.where((lane >= j * SLOT) & (lane < (j + 1) * SLOT), one, mixed)
            col_sum = jnp.sum(mixed, axis=0, keepdims=True)
            col_parts[k] = col_sum if col_parts[k] is None else col_parts[k] + col_sum
            turned = mixed.T
            base[k * 128:(k + 1) * 128, part * half:(part + 1) * half] = turned
            row_part = turned if row_part is None else row_part + turned
        cs[part] = sum(row_part[j * SLOT:(j + 1) * SLOT] for j in range(PACK))
        for off in dept_order[:-1]:
            send_cs(off, part).start()

    block = STORES_IN_CHUNK * items
    blocks = stores // STORES_IN_CHUNK
    blocks_in_half = half // STORES_IN_CHUNK
    scale(0, 2 * block)
    for number in range(0, blocks - 2, 2):
        def step(i, carry, number=number):
            starts = [(number + i) * block + part * (block // 2) for part in range(2)]
            pieces = [pl.ds(pl.multiple_of(start, SCALED_ROWS), block // 2) for start in starts]
            for rows, result in zip(pieces, layers([scaled[rows, :] for rows in pieces], w1, w2, w3)):
                flat[rows, :] = result * flat[rows, :]
            return carry

        lax.fori_loop(0, 2, step, 0)
        scale((number + 2) * block, 2 * block)
        if number == 0:
            for m in range(1, pairs):
                send_pair(m).wait_recv()
                store_sums[dept_at(2 * m)] = store_sums[dept_at(2 * m)] + pair_recv[m]
                send_store(m).start()
        if (number + 2) % blocks_in_half == 0:
            turn((number + 2) // blocks_in_half - 1)

    run((blocks - 2) * block, [block // 2, block // 2])

    sum_rows[own:, :] = jnp.zeros((sum_rows.shape[0] - own, days), F32)
    send_pair(0).wait_recv()
    store_total = store_sums[my_dept] + pair_recv[0]
    for m in range(1, pairs):
        send_store(m).wait_recv()
        store_total = store_total + store_recv[m]
    sum_rows[0:own, :] = store_total
    item_total = item_sums[my_store]
    for off in range(1, n_store):
        send_item(off).wait_recv()
        item_total = item_total + item_recv[off]
    sum_rows[own:own + item_share, :] = item_total
    upper_mean = scales(sum_rows[...])
    upper_scaled = (sum_rows[...] * (1.0 / upper_mean)).astype(BF16)
    (upper,) = run((blocks - 1) * block, [block], [upper_scaled])
    upper = upper * upper_mean
    up[...] = jnp.concatenate([upper[:own]] * (128 // own), axis=0).T[:SLOT]
    for off in dept_order[:-1]:
        send_up(off).start()

    turn(stores // half - 1)
    write_base = pltpu.make_async_copy(base, base_out, out_sem.at[0])
    write_base.start()

    packed = lax.broadcasted_iota(jnp.int32, ci.shape, 0) * PACK
    packed_lane = lax.broadcasted_iota(jnp.int32, ci.shape, 1)
    for j in range(1, PACK):
        packed = packed + (packed_lane >= j * SLOT).astype(jnp.int32)
    ci[...] = jnp.zeros_like(ci)
    for k in range(groups):
        ci[k:k + 1, :] = 0.0 - col_parts[k]
    ci_mine = ci[...]
    for t in range(item_share):
        number = my_store * item_share + t
        ci_mine = ci_mine + jnp.where((packed == number) & (packed < items), upper[own + t:own + t + 1], 0.0)
    base_total = sum(col_parts)
    base_total = base_total + pltpu.roll(base_total, 2 * SLOT, 1)
    base_total = base_total + pltpu.roll(base_total, SLOT, 1)
    ci[...] = ci_mine
    ci[groups:groups + 1, :] = jnp.sum(upper[:own], axis=0, keepdims=True) - base_total
    ci[groups + 1:groups + 2, :] = jnp.sum(upper[own:own + item_share], axis=0, keepdims=True) - base_total

    def send_ci(off):
        return pltpu.make_async_remote_copy(
            src_ref=ci, dst_ref=ci_recv.at[off], send_sem=ci_send.at[off], recv_sem=ci_get.at[off],
            device_id=(store_at(off), my_dept), device_id_type=MESH,
        )

    def send_err(off):
        return pltpu.make_async_remote_copy(
            src_ref=err, dst_ref=err_recv.at[off], send_sem=err_send.at[off], recv_sem=err_get.at[off],
            device_id=(my_store, dept_at(off)), device_id_type=MESH,
        )

    for off in range(1, n_store):
        send_ci(off).start()

    item_err = ci[...]
    for off in range(1, n_store):
        send_ci(off).wait_recv()
        item_err = item_err + ci_recv[off]

    err[...] = item_err[groups:groups + 2]
    for off in range(1, n_dept):
        send_err(off).start()

    place = lax.broadcasted_iota(jnp.int32, (SLOT, stores), 1)

    def placed(piece, owner):
        mine = (place >= owner * own) & (place < (owner + 1) * own)
        return jnp.where(mine, jnp.concatenate([piece] * (stores // 128), axis=1), 0.0)

    store_parts = [cs[part] for part in range(stores // half)]
    store_err = placed(up[...], my_dept)
    for off in range(1, n_dept):
        for part in range(stores // half):
            send_cs(off, part).wait_recv()
            store_parts[part] = store_parts[part] + cs_recv[off, part]
        send_up(off).wait_recv()
        store_err = store_err + placed(up_recv[off], dept_at(n_dept - off))
    store_err = store_err - jnp.concatenate(store_parts, axis=1)
    errs = err[...]
    for off in range(1, n_dept):
        send_err(off).wait_recv()
        errs = errs + err_recv[off]
    err_s, err_i = errs[0:1], errs[1:2]
    item_count = float(items * n_dept)
    store_count = float(stores * n_store)
    denominator = 1.0 + item_count + store_count
    shift_s = (err_s * (1.0 + store_count) - store_count * err_i) / denominator
    shift_i = ((1.0 + item_count) * err_i - item_count * err_s) / denominator
    shift_i_col = jnp.broadcast_to(shift_i, (128, 128)).T[:SLOT]
    shift_i_all = jnp.concatenate([shift_i_col] * (stores // 128), axis=1)
    small[0:SLOT, :] = (store_err - shift_i_all) * (1.0 / (1.0 + item_count))
    small[SLOT:2 * SLOT, :] = store_err * (1.0 / math.sqrt(item_count))
    small[2 * SLOT:, 0:128] = (item_err - shift_s) * (1.0 / (1.0 + store_count))
    small[2 * SLOT:, 128:256] = item_err * (1.0 / math.sqrt(store_count))
    write_small = pltpu.make_async_copy(small, small_out, out_sem.at[1])
    write_small.start()

    for off in range(1, n_dept):
        send_up(off).wait_send()
        send_err(off).wait_send()
        for part in range(stores // half):
            send_cs(off, part).wait_send()
    for m in range(pairs):
        send_pair(m).wait_send()
        if m:
            send_store(m).wait_send()
    for off in range(1, n_store):
        send_item(off).wait_send()
        send_ci(off).wait_send()
    write_base.wait()
    write_small.wait()


def final_kernel(
    items, horizon, base_hbm, small_hbm, reconciled_out, store_gap_out, item_gap_out,
    base, small, reconciled, store_gap, item_gap, read_sem, write_sem,
):
    groups = base.shape[0] // 128
    read_small = pltpu.make_async_copy(small_hbm, small, read_sem.at[groups])
    read_small.start()
    reads, writes = [], []
    for k in range(groups):
        rows = pl.ds(k * 128, 128)
        reads.append(pltpu.make_async_copy(base_hbm.at[rows], base.at[rows], read_sem.at[k]))
        reads[k].start()
    read_small.wait()
    shift = small[0:SLOT, :]
    item_shift = small[2 * SLOT:, 0:128]
    gap = small[2 * SLOT:, 128:256]
    columns = jnp.concatenate([item_shift] + [jnp.zeros((128 - item_shift.shape[0], 128), F32)], axis=0).T
    store_gap[...] = small[SLOT:SLOT + horizon, :]
    for item in range(items):
        k, j = divmod(item, PACK)
        item_gap[item:item + 1, :] = gap[k:k + 1, j * SLOT:j * SLOT + horizon]
    writes.append(pltpu.make_async_copy(store_gap, store_gap_out, write_sem.at[groups]))
    writes.append(pltpu.make_async_copy(item_gap, item_gap_out, write_sem.at[groups + 1]))
    writes[0].start()
    writes[1].start()
    for k in range(groups):
        reads[k].wait()
        mine = range(k * PACK, min((k + 1) * PACK, items))
        for item in mine:
            j = item - k * PACK
            first = k * 128 + j * SLOT
            block = base[first:first + SLOT, :] + shift + columns[j * SLOT:(j + 1) * SLOT, k:k + 1]
            reconciled[item * horizon:(item + 1) * horizon, :] = block[:horizon]
        rows = pl.ds(mine[0] * horizon, len(mine) * horizon)
        writes.append(pltpu.make_async_copy(reconciled.at[rows], reconciled_out.at[rows], write_sem.at[k]))
        writes[-1].start()
    for write in writes:
        write.wait()


def body(n_store, n_dept, history, input_layer_matrix, middle_layer_matrix, final_layer_matrix):
    stores, items, days = history.shape
    hidden = input_layer_matrix.shape[1]
    horizon = final_layer_matrix.shape[1]
    own = stores // n_dept
    item_share = -(-items // n_store)
    groups = -(-items // PACK)
    group_rows = -(-(groups + 2) // 8) * 8
    share_rows = -(-item_share // 8) * 8
    in_hbm = pl.BlockSpec(memory_space=pl.ANY)
    dma = pltpu.SemaphoreType.DMA
    shape = jax.ShapeDtypeStruct
    parts = pl.pallas_call(
        functools.partial(main_kernel, n_store, n_dept, stores, items, horizon),
        out_shape=(
            shape((groups * 128, stores), F32),
            shape((2 * SLOT + group_rows, stores), F32),
        ),
        in_specs=[in_hbm] * 4,
        out_specs=[in_hbm] * 2,
        scratch_shapes=[
            pltpu.VMEM((groups * 128, stores), F32),
            pltpu.VMEM((2 * SLOT + group_rows, stores), F32),
            pltpu.VMEM((stores * items, days), BF16),
            pltpu.VMEM((stores * items, days), BF16),
            pltpu.VMEM((days, hidden), BF16),
            pltpu.VMEM((hidden, hidden), BF16),
            pltpu.VMEM((horizon, hidden), BF16),
            pltpu.VMEM((128, hidden), F32),
            pltpu.VMEM((hidden, 128), BF16),
            pltpu.VMEM((own + items, own * items), BF16),
            pltpu.VMEM((n_dept, own, days), F32),
            pltpu.VMEM((n_dept // 2, own, days), F32),
            pltpu.VMEM((n_dept // 2, own, days), F32),
            pltpu.VMEM((-(-n_store * item_share // 8) * 8, days), F32),
            pltpu.VMEM((n_store, item_share, days), F32),
            pltpu.VMEM((n_store, item_share, days), F32),
            pltpu.VMEM((own + share_rows, days), F32),
            pltpu.VMEM((stores * items, 128), F32),
            pltpu.VMEM((stores // 128, SLOT, 128), F32),
            pltpu.VMEM((n_dept, stores // 128, SLOT, 128), F32),
            pltpu.VMEM((SLOT, 128), F32),
            pltpu.VMEM((n_dept, SLOT, 128), F32),
            pltpu.VMEM((group_rows, 128), F32),
            pltpu.VMEM((n_store, group_rows, 128), F32),
            pltpu.VMEM((2, 128), F32),
            pltpu.VMEM((n_dept, 2, 128), F32),
            dma((n_dept,)),
            dma((3,)),
            dma((n_dept // 2,)),
            dma((n_dept // 2,)),
            dma((n_dept // 2,)),
            dma((n_dept // 2,)),
            dma((n_store,)),
            dma((n_store,)),
            dma((n_dept, stores // 128)),
            dma((n_dept, stores // 128)),
            dma((n_dept,)),
            dma((n_dept,)),
            dma((n_store,)),
            dma((n_store,)),
            dma((n_dept,)),
            dma((n_dept,)),
            dma((2,)),
        ],
        compiler_params=pltpu.CompilerParams(
            collective_id=0, has_side_effects=True, vmem_limit_bytes=60 * 2**20
        ),
    )(
        history.reshape(stores * items, days),
        input_layer_matrix,
        middle_layer_matrix,
        final_layer_matrix.T,
    )
    reconciled, store_gap, item_gap = pl.pallas_call(
        functools.partial(final_kernel, items, horizon),
        out_shape=(
            shape((items * horizon, stores), F32),
            shape((horizon, stores), F32),
            shape((items, horizon), F32),
        ),
        in_specs=[in_hbm] * 2,
        out_specs=[in_hbm] * 3,
        scratch_shapes=[
            pltpu.VMEM((groups * 128, stores), F32),
            pltpu.VMEM((2 * SLOT + group_rows, stores), F32),
            pltpu.VMEM((items * horizon, stores), F32),
            pltpu.VMEM((horizon, stores), F32),
            pltpu.VMEM((items, horizon), F32),
            dma((groups + 1,)),
            dma((groups + 2,)),
        ],
        compiler_params=pltpu.CompilerParams(vmem_limit_bytes=60 * 2**20),
    )(*parts)
    return reconciled.T, store_gap, item_gap.T


def solution(mesh):
    return jax.shard_map(
        functools.partial(body, mesh.shape["store"], mesh.shape["dept"]),
        mesh=mesh,
        in_specs=(P("store", "dept", None), P(), P(), P()),
        out_specs=(P("store", "dept"), P(None, "store"), P(None, "dept")),
        check_vma=False,
    )
```

```python
import functools
import math

import jax
import jax.numpy as jnp
from jax import lax
from jax.experimental import pallas as pl
from jax.experimental.pallas import tpu as pltpu
from jax.sharding import PartitionSpec as P

MESH = pl.DeviceIdType.MESH
F32 = jnp.float32
BF16 = jnp.bfloat16
SLOT = 32
PACK = 4
STORES_IN_CHUNK = 32
SCALED_ROWS = 128


def scales(values):
    mean = jnp.sum(values * values, axis=-1, keepdims=True) * (1.0 / values.shape[-1])
    return jnp.sqrt(mean + 1e-05)


def layers(blocks, w1, w2, w3):
    for weights in (w1, w2):
        blocks = [jnp.dot(block, weights[...], preferred_element_type=F32).astype(BF16) for block in blocks]
        blocks = [jnp.maximum(block, 0) for block in blocks]
    return [jnp.dot(block, w3[...], preferred_element_type=F32) for block in blocks]


def main_kernel(
    n_store, n_dept, stores, items, horizon,
    hist_hbm, w1_hbm, w2_hbm, w3_hbm,
    base_out, small_out,
    base, small, hist, scaled, w1, w2, w3_narrow, w3_wide, w3, selector, store_sums, pair_recv, store_recv, item_acc, item_sums, item_recv,
    sum_rows, flat, cs, cs_recv, up, up_recv, ci, ci_recv, err, err_recv,
    hist_sem, weight_sem, sp_send, sp_get, ss_send, ss_get, is_send, is_get, cs_send, cs_get, up_send, up_get,
    ci_send, ci_get, err_send, err_get, out_sem,
):
    my_store = lax.axis_index("store")
    my_dept = lax.axis_index("dept")
    own = stores // n_dept
    own_rows = own * items
    days = hist.shape[1]
    item_share = item_sums.shape[1]
    groups = -(-items // PACK)
    dept_order = sorted(range(1, n_dept), key=lambda o: -min(o, n_dept - o)) + [0]

    def dept_at(off):
        return lax.rem(my_dept + off, n_dept)

    def store_at(off):
        return lax.rem(my_store + off, n_store)

    def rows_of(chunk):
        return pl.ds(pl.multiple_of(chunk * own_rows, own_rows), own_rows)

    def load_chunk(slot, chunk):
        rows = rows_of(chunk)
        return pltpu.make_async_copy(hist_hbm.at[rows], hist.at[rows], hist_sem.at[slot])

    early = lax.rem(my_dept + 1, 2) + my_dept - lax.rem(my_dept, 2)
    for slot in range(n_dept):
        near = slot % (n_dept // 2) == n_dept // 2 - 1
        ahead = 0 if near else 2 * (slot % (n_dept // 2) + 1)
        load_chunk(slot, lax.rem((early if slot < n_dept // 2 else my_dept) + ahead, n_dept)).start()
    load_w1 = pltpu.make_async_copy(w1_hbm, w1, weight_sem.at[0])
    load_w2 = pltpu.make_async_copy(w2_hbm, w2, weight_sem.at[1])
    load_w3 = pltpu.make_async_copy(w3_hbm, w3_narrow, weight_sem.at[2])
    load_w3.start()
    load_w1.start()
    load_w2.start()

    barrier = pltpu.get_barrier_semaphore()

    for off in range(1, n_dept):
        pl.semaphore_signal(barrier, inc=1, device_id=(my_store, dept_at(off)), device_id_type=MESH)
    for off in range(1, n_store):
        pl.semaphore_signal(barrier, inc=1, device_id=(store_at(off), my_dept), device_id_type=MESH)

    row = lax.broadcasted_iota(jnp.int32, selector.shape, 0)
    col = lax.broadcasted_iota(jnp.int32, selector.shape, 1)
    of_store = (col >= row * items) & (col < row * items + items)
    col_f = col.astype(F32)
    which = col_f - items * jnp.floor((col_f + 0.5) * (1.0 / items))
    of_item = which == (row - own).astype(F32)
    selector[...] = jnp.where(row < own, of_store.astype(F32), of_item.astype(F32)).astype(BF16)

    w3_wide[...] = jnp.zeros_like(w3_wide)
    load_w3.wait()
    last_layer = w3_narrow[...].astype(F32)
    for j in range(PACK):
        w3_wide[j * SLOT:j * SLOT + horizon, :] = last_layer
    w3[...] = w3_wide[...].T.astype(BF16)

    pl.semaphore_wait(barrier, n_dept + n_store - 2)

    partner = my_dept + 1 - 2 * lax.rem(my_dept, 2)
    pairs = n_dept // 2

    def partner_block(m):
        return lax.rem(partner + 2 * m, n_dept)

    def send_pair(m):
        return pltpu.make_async_remote_copy(
            src_ref=store_sums.at[partner_block(m)], dst_ref=pair_recv.at[m],
            send_sem=sp_send.at[m], recv_sem=sp_get.at[m],
            device_id=(my_store, partner), device_id_type=MESH,
        )

    def send_store(m):
        return pltpu.make_async_remote_copy(
            src_ref=store_sums.at[dept_at(2 * m)], dst_ref=store_recv.at[m],
            send_sem=ss_send.at[m], recv_sem=ss_get.at[m],
            device_id=(my_store, dept_at(2 * m)), device_id_type=MESH,
        )

    def send_item(off):
        return pltpu.make_async_remote_copy(
            src_ref=item_sums.at[store_at(off)], dst_ref=item_recv.at[off],
            send_sem=is_send.at[off], recv_sem=is_get.at[off],
            device_id=(store_at(off), my_dept), device_id_type=MESH,
        )

    item_total = None
    far_first = list(range(1, pairs)) + [0]
    for slot, (m, sent) in enumerate([(m, True) for m in far_first] + [(m, False) for m in far_first]):
        chunk = partner_block(m) if sent else dept_at(2 * m)
        load_chunk(slot, chunk).wait()
        sums = jnp.dot(selector[...], hist[rows_of(chunk), :], preferred_element_type=F32)
        store_sums[chunk] = sums[:own]
        if sent:
            send_pair(m).start()
        item_total = sums[own:] if item_total is None else item_total + sums[own:]
    item_acc[...] = jnp.zeros_like(item_acc)
    item_acc[0:items, :] = item_total
    for place in range(n_store):
        item_sums[place] = item_acc[place * item_share:(place + 1) * item_share, :]
    for off in range(1, n_store):
        send_item(off).start()

    load_w1.wait()
    load_w2.wait()
    half = 128
    lane = lax.broadcasted_iota(jnp.int32, (half, 128), 1)
    col_parts = [None] * groups

    def send_cs(off, part):
        return pltpu.make_async_remote_copy(
            src_ref=cs.at[part], dst_ref=cs_recv.at[off, part],
            send_sem=cs_send.at[off, part], recv_sem=cs_get.at[off, part],
            device_id=(my_store, dept_at(off)), device_id_type=MESH,
        )

    def send_up(off):
        return pltpu.make_async_remote_copy(
            src_ref=up, dst_ref=up_recv.at[off], send_sem=up_send.at[off], recv_sem=up_get.at[off],
            device_id=(my_store, dept_at(off)), device_id_type=MESH,
        )

    def scale(first, count):
        for start in range(first, first + count, SCALED_ROWS):
            rows = slice(start, start + SCALED_ROWS)
            root_mean = scales(hist[rows, :].astype(F32))
            flat[rows, :] = jnp.broadcast_to(root_mean, (SCALED_ROWS, 128))
            scaled[rows, :] = (hist[rows, :].astype(F32) * (1.0 / root_mean)).astype(BF16)

    def run(first, sizes, more=()):
        starts = [first + sum(sizes[:i]) for i in range(len(sizes))]
        pieces = [slice(start, start + size) for start, size in zip(starts, sizes)]
        results = layers(list(more) + [scaled[rows, :] for rows in pieces], w1, w2, w3)
        for rows, result in zip(pieces, results[len(more):]):
            flat[rows, :] = result * flat[rows, :]
        return results[:len(more)]

    def turn(part):
        row_part = None
        for k in range(groups):
            mixed = jnp.zeros((half, 128), F32)
            for j in range(PACK):
                if k * PACK + j < items:
                    one = flat[pl.ds(part * half * items + k * PACK + j, half, stride=items), :]
                    mixed = jnp.where((lane >= j * SLOT) & (lane < (j + 1) * SLOT), one, mixed)
            col_sum = jnp.sum(mixed, axis=0, keepdims=True)
            col_parts[k] = col_sum if col_parts[k] is None else col_parts[k] + col_sum
            turned = mixed.T
            base[k * 128:(k + 1) * 128, part * half:(part + 1) * half] = turned
            row_part = turned if row_part is None else row_part + turned
        cs[part] = sum(row_part[j * SLOT:(j + 1) * SLOT] for j in range(PACK))
        for off in dept_order[:-1]:
            send_cs(off, part).start()

    block = STORES_IN_CHUNK * items
    blocks = stores // STORES_IN_CHUNK
    blocks_in_half = half // STORES_IN_CHUNK
    scale(0, 2 * block)
    for number in range(0, blocks - 2, 2):
        run(number * block, [block, block])
        scale((number + 2) * block, 2 * block)
        if number == 0:
            for m in range(1, pairs):
                send_pair(m).wait_recv()
                store_sums[dept_at(2 * m)] = store_sums[dept_at(2 * m)] + pair_recv[m]
                send_store(m).start()
        if (number + 2) % blocks_in_half == 0:
            turn((number + 2) // blocks_in_half - 1)

    run((blocks - 2) * block, [block, block])
    turn(stores // half - 1)
    write_base = pltpu.make_async_copy(base, base_out, out_sem.at[0])
    write_base.start()

    sum_rows[own:, :] = jnp.zeros((sum_rows.shape[0] - own, days), F32)
    send_pair(0).wait_recv()
    store_total = store_sums[my_dept] + pair_recv[0]
    for m in range(1, pairs):
        send_store(m).wait_recv()
        store_total = store_total + store_recv[m]
    sum_rows[0:own, :] = store_total
    item_total = item_sums[my_store]
    for off in range(1, n_store):
        send_item(off).wait_recv()
        item_total = item_total + item_recv[off]
    sum_rows[own:own + item_share, :] = item_total
    upper_mean = scales(sum_rows[...])
    upper_scaled = (sum_rows[...] * (1.0 / upper_mean)).astype(BF16)
    (upper,) = layers([upper_scaled], w1, w2, w3)
    upper = upper * upper_mean
    up[...] = jnp.concatenate([upper[:own]] * (128 // own), axis=0).T[:SLOT]
    for off in dept_order[:-1]:
        send_up(off).start()


    packed = lax.broadcasted_iota(jnp.int32, ci.shape, 0) * PACK
    packed_lane = lax.broadcasted_iota(jnp.int32, ci.shape, 1)
    for j in range(1, PACK):
        packed = packed + (packed_lane >= j * SLOT).astype(jnp.int32)
    ci[...] = jnp.zeros_like(ci)
    for k in range(groups):
        ci[k:k + 1, :] = 0.0 - col_parts[k]
    ci_mine = ci[...]
    for t in range(item_share):
        number = my_store * item_share + t
        ci_mine = ci_mine + jnp.where((packed == number) & (packed < items), upper[own + t:own + t + 1], 0.0)
    base_total = sum(col_parts)
    base_total = base_total + pltpu.roll(base_total, 2 * SLOT, 1)
    base_total = base_total + pltpu.roll(base_total, SLOT, 1)
    ci[...] = ci_mine
    ci[groups:groups + 1, :] = jnp.sum(upper[:own], axis=0, keepdims=True) - base_total
    ci[groups + 1:groups + 2, :] = jnp.sum(upper[own:own + item_share], axis=0, keepdims=True) - base_total

    def send_ci(off):
        return pltpu.make_async_remote_copy(
            src_ref=ci, dst_ref=ci_recv.at[off], send_sem=ci_send.at[off], recv_sem=ci_get.at[off],
            device_id=(store_at(off), my_dept), device_id_type=MESH,
        )

    def send_err(off):
        return pltpu.make_async_remote_copy(
            src_ref=err, dst_ref=err_recv.at[off], send_sem=err_send.at[off], recv_sem=err_get.at[off],
            device_id=(my_store, dept_at(off)), device_id_type=MESH,
        )

    for off in range(1, n_store):
        send_ci(off).start()

    item_err = ci[...]
    for off in range(1, n_store):
        send_ci(off).wait_recv()
        item_err = item_err + ci_recv[off]

    err[...] = item_err[groups:groups + 2]
    for off in range(1, n_dept):
        send_err(off).start()

    place = lax.broadcasted_iota(jnp.int32, (SLOT, stores), 1)

    def placed(piece, owner):
        mine = (place >= owner * own) & (place < (owner + 1) * own)
        return jnp.where(mine, jnp.concatenate([piece] * (stores // 128), axis=1), 0.0)

    store_parts = [cs[part] for part in range(stores // half)]
    store_err = placed(up[...], my_dept)
    for off in range(1, n_dept):
        for part in range(stores // half):
            send_cs(off, part).wait_recv()
            store_parts[part] = store_parts[part] + cs_recv[off, part]
        send_up(off).wait_recv()
        store_err = store_err + placed(up_recv[off], dept_at(n_dept - off))
    store_err = store_err - jnp.concatenate(store_parts, axis=1)
    errs = err[...]
    for off in range(1, n_dept):
        send_err(off).wait_recv()
        errs = errs + err_recv[off]
    err_s, err_i = errs[0:1], errs[1:2]
    item_count = float(items * n_dept)
    store_count = float(stores * n_store)
    denominator = 1.0 + item_count + store_count
    shift_s = (err_s * (1.0 + store_count) - store_count * err_i) / denominator
    shift_i = ((1.0 + item_count) * err_i - item_count * err_s) / denominator
    shift_i_col = jnp.broadcast_to(shift_i, (128, 128)).T[:SLOT]
    shift_i_all = jnp.concatenate([shift_i_col] * (stores // 128), axis=1)
    small[0:SLOT, :] = (store_err - shift_i_all) * (1.0 / (1.0 + item_count))
    small[SLOT:2 * SLOT, :] = store_err * (1.0 / math.sqrt(item_count))
    small[2 * SLOT:, 0:128] = (item_err - shift_s) * (1.0 / (1.0 + store_count))
    small[2 * SLOT:, 128:256] = item_err * (1.0 / math.sqrt(store_count))
    write_small = pltpu.make_async_copy(small, small_out, out_sem.at[1])
    write_small.start()

    for off in range(1, n_dept):
        send_up(off).wait_send()
        send_err(off).wait_send()
        for part in range(stores // half):
            send_cs(off, part).wait_send()
    for m in range(pairs):
        send_pair(m).wait_send()
        if m:
            send_store(m).wait_send()
    for off in range(1, n_store):
        send_item(off).wait_send()
        send_ci(off).wait_send()
    write_base.wait()
    write_small.wait()


def final_kernel(
    items, horizon, base_hbm, small_hbm, reconciled_out, store_gap_out, item_gap_out,
    base, small, reconciled, store_gap, item_gap, read_sem, write_sem,
):
    groups = base.shape[0] // 128
    read_small = pltpu.make_async_copy(small_hbm, small, read_sem.at[groups])
    read_small.start()
    reads, writes = [], []
    for k in range(groups):
        rows = pl.ds(k * 128, 128)
        reads.append(pltpu.make_async_copy(base_hbm.at[rows], base.at[rows], read_sem.at[k]))
        reads[k].start()
    read_small.wait()
    shift = small[0:SLOT, :]
    item_shift = small[2 * SLOT:, 0:128]
    gap = small[2 * SLOT:, 128:256]
    columns = jnp.concatenate([item_shift] + [jnp.zeros((128 - item_shift.shape[0], 128), F32)], axis=0).T
    store_gap[...] = small[SLOT:SLOT + horizon, :]
    for item in range(items):
        k, j = divmod(item, PACK)
        item_gap[item:item + 1, :] = gap[k:k + 1, j * SLOT:j * SLOT + horizon]
    writes.append(pltpu.make_async_copy(store_gap, store_gap_out, write_sem.at[groups]))
    writes.append(pltpu.make_async_copy(item_gap, item_gap_out, write_sem.at[groups + 1]))
    writes[0].start()
    writes[1].start()
    for k in range(groups):
        reads[k].wait()
        mine = range(k * PACK, min((k + 1) * PACK, items))
        for item in mine:
            j = item - k * PACK
            first = k * 128 + j * SLOT
            block = base[first:first + SLOT, :] + shift + columns[j * SLOT:(j + 1) * SLOT, k:k + 1]
            reconciled[item * horizon:(item + 1) * horizon, :] = block[:horizon]
        rows = pl.ds(mine[0] * horizon, len(mine) * horizon)
        writes.append(pltpu.make_async_copy(reconciled.at[rows], reconciled_out.at[rows], write_sem.at[k]))
        writes[-1].start()
    for write in writes:
        write.wait()


def body(n_store, n_dept, history, input_layer_matrix, middle_layer_matrix, final_layer_matrix):
    stores, items, days = history.shape
    hidden = input_layer_matrix.shape[1]
    horizon = final_layer_matrix.shape[1]
    own = stores // n_dept
    item_share = -(-items // n_store)
    groups = -(-items // PACK)
    group_rows = -(-(groups + 2) // 8) * 8
    share_rows = -(-item_share // 8) * 8
    in_hbm = pl.BlockSpec(memory_space=pl.ANY)
    dma = pltpu.SemaphoreType.DMA
    shape = jax.ShapeDtypeStruct
    parts = pl.pallas_call(
        functools.partial(main_kernel, n_store, n_dept, stores, items, horizon),
        out_shape=(
            shape((groups * 128, stores), F32),
            shape((2 * SLOT + group_rows, stores), F32),
        ),
        in_specs=[in_hbm] * 4,
        out_specs=[in_hbm] * 2,
        scratch_shapes=[
            pltpu.VMEM((groups * 128, stores), F32),
            pltpu.VMEM((2 * SLOT + group_rows, stores), F32),
            pltpu.VMEM((stores * items, days), BF16),
            pltpu.VMEM((stores * items, days), BF16),
            pltpu.VMEM((days, hidden), BF16),
            pltpu.VMEM((hidden, hidden), BF16),
            pltpu.VMEM((horizon, hidden), BF16),
            pltpu.VMEM((128, hidden), F32),
            pltpu.VMEM((hidden, 128), BF16),
            pltpu.VMEM((own + items, own * items), BF16),
            pltpu.VMEM((n_dept, own, days), F32),
            pltpu.VMEM((n_dept // 2, own, days), F32),
            pltpu.VMEM((n_dept // 2, own, days), F32),
            pltpu.VMEM((-(-n_store * item_share // 8) * 8, days), F32),
            pltpu.VMEM((n_store, item_share, days), F32),
            pltpu.VMEM((n_store, item_share, days), F32),
            pltpu.VMEM((own + share_rows, days), F32),
            pltpu.VMEM((stores * items, 128), F32),
            pltpu.VMEM((stores // 128, SLOT, 128), F32),
            pltpu.VMEM((n_dept, stores // 128, SLOT, 128), F32),
            pltpu.VMEM((SLOT, 128), F32),
            pltpu.VMEM((n_dept, SLOT, 128), F32),
            pltpu.VMEM((group_rows, 128), F32),
            pltpu.VMEM((n_store, group_rows, 128), F32),
            pltpu.VMEM((2, 128), F32),
            pltpu.VMEM((n_dept, 2, 128), F32),
            dma((n_dept,)),
            dma((3,)),
            dma((n_dept // 2,)),
            dma((n_dept // 2,)),
            dma((n_dept // 2,)),
            dma((n_dept // 2,)),
            dma((n_store,)),
            dma((n_store,)),
            dma((n_dept, stores // 128)),
            dma((n_dept, stores // 128)),
            dma((n_dept,)),
            dma((n_dept,)),
            dma((n_store,)),
            dma((n_store,)),
            dma((n_dept,)),
            dma((n_dept,)),
            dma((2,)),
        ],
        compiler_params=pltpu.CompilerParams(
            collective_id=0, has_side_effects=True, vmem_limit_bytes=60 * 2**20
        ),
    )(
        history.reshape(stores * items, days),
        input_layer_matrix,
        middle_layer_matrix,
        final_layer_matrix.T,
    )
    reconciled, store_gap, item_gap = pl.pallas_call(
        functools.partial(final_kernel, items, horizon),
        out_shape=(
            shape((items * horizon, stores), F32),
            shape((horizon, stores), F32),
            shape((items, horizon), F32),
        ),
        in_specs=[in_hbm] * 2,
        out_specs=[in_hbm] * 3,
        scratch_shapes=[
            pltpu.VMEM((groups * 128, stores), F32),
            pltpu.VMEM((2 * SLOT + group_rows, stores), F32),
            pltpu.VMEM((items * horizon, stores), F32),
            pltpu.VMEM((horizon, stores), F32),
            pltpu.VMEM((items, horizon), F32),
            dma((groups + 1,)),
            dma((groups + 2,)),
        ],
        compiler_params=pltpu.CompilerParams(vmem_limit_bytes=60 * 2**20),
    )(*parts)
    return reconciled.T, store_gap, item_gap.T


def solution(mesh):
    return jax.shard_map(
        functools.partial(body, mesh.shape["store"], mesh.shape["dept"]),
        mesh=mesh,
        in_specs=(P("store", "dept", None), P(), P(), P()),
        out_specs=(P("store", "dept"), P(None, "store"), P(None, "dept")),
        check_vma=False,
    )
```
